256 devices in a mesh: lead: 16 (over x, z_lo), space: 16 (over z_hi, y, core).
Axes of the slice: x: 4, y: 4, z: 8 (z_hi: 2, z_lo: 4; z = z_hi * 4 + z_lo), core: 2. Of those that a mesh axis runs over, the one named last changes fastest.
Arguments:
- latents: bfloat16 [16, 64, 128, 1024], P('lead', 'space'), may hold values from -6 to 6
- owners: int32 [2], replicated, may hold values from 0 to 15, as said below
- lead_ids: int32 [16], P('lead'), may hold values from 0 to 359
- film_scale: float32 [360, 1024], replicated, may hold values from -3 to 3
- film_shift: float32 [360, 1024], replicated, may hold values from -3 to 3
- w_qkv_row: bfloat16 [1024, 3072], P('space'), may hold values from -0.1875 to 0.1875
- w_out_row: bfloat16 [1024, 1024], P('space'), may hold values from -0.1875 to 0.1875
- gain_col: float32 [1024], replicated, may hold values from 0.25 to 1.75
- w_qkv_col: bfloat16 [1024, 3072], P('space'), may hold values from -0.1875 to 0.1875
- w_out_col: bfloat16 [1024, 1024], P('space'), may hold values from -0.1875 to 0.1875
Outputs:
- result: bfloat16 [16, 64, 128, 1024], P('lead', None, 'space')
The draws below stay inside these ranges and needn't reach their ends.
Inputs may be any that keep to these rules, and one draw needn't show every extreme that they name: `owners`: the two analysis times are held by two different lead groups, one of which is the last lead group.
All inputs are finite; a program needn't handle non-finite values.
Results may differ from the reference program's by a relative error of at most 0.013.
Values may be sent and summed in bfloat16 or wider, within the bound.
A program may use at most 64 MiB of HBM per device.

```python
import jax
import jax.numpy as jnp
from jax import lax

C = 1024
HEADS = 8
H = 64
W = 128
NLEADS = 360
N_LEAD = 16


def draw_owners(key, part):
    other = jax.random.randint(jax.random.fold_in(key, 11), (), 0, N_LEAD - 1).astype(jnp.int32)
    last = jnp.int32(N_LEAD - 1)
    flip = jax.random.randint(jax.random.fold_in(key, 12), (), 0, 2).astype(jnp.int32)
    first = jnp.where(flip == 1, last, other)
    second = jnp.where(flip == 1, other, last)
    return jnp.stack([first, second]).astype(jnp.int32)


def with_ends(result, key, low, high):
    dims = result.shape
    place = [jax.random.randint(jax.random.fold_in(key, axis), (), 0, dims[axis]) for axis in range(len(dims))]
    result = result.at[tuple(place)].set(low)
    longest = dims.index(max(dims))
    place[longest] = (place[longest] + 1) % dims[longest]
    return result.at[tuple(place)].set(high)


def level_of(key, extent, cuts, least, largest):
    factor_of = 1.0
    for dim, shards_of in cuts:
        steps = jax.random.uniform(jax.random.fold_in(jax.random.fold_in(key, 6), dim), (shards_of,), jnp.float32, least / len(cuts), largest / len(cuts))
        factor_of = factor_of * jnp.repeat(jnp.exp(steps), extent[dim] // shards_of).reshape((-1,) + (1,) * (len(extent) - 1 - dim))
    return factor_of


def centred(stream_key, shape, scale, bound, shards=(), kind=jnp.bfloat16):
    array = jax.random.normal(stream_key, shape, jnp.float32) * scale
    if len(shards) > 0:
        array = level_of(stream_key, shape, shards, -0.22, 0.18) * array
    return jnp.clip(array, min=-bound, max=bound).astype(kind)


def setup_inputs(seed: int = 0) -> dict:
    seeds = jax.random.split(jax.random.key(seed), 11)
    return {
        "latents": centred(seeds[0], (N_LEAD, H, W, C), 1.0, 6.0, ((0, 16), (1, 16))),
        "owners": draw_owners(jax.random.fold_in(seeds[10], 71), 0),
        "lead_ids": with_ends(jax.random.randint(seeds[2], (N_LEAD,), 0, NLEADS), jax.random.fold_in(seeds[2], 1), 0, NLEADS - 1).astype(jnp.int32),
        "film_scale": centred(seeds[3], (NLEADS, C), 0.5, 3.0, (), jnp.float32),
        "film_shift": centred(seeds[4], (NLEADS, C), 0.5, 3.0, (), jnp.float32),
        "w_qkv_row": centred(seeds[5], (C, 3 * C), C ** -0.5, 0.1875, ((0, 16),)),
        "w_out_row": centred(seeds[6], (C, C), C ** -0.5, 0.1875, ((0, 16),)),
        "gain_col": jnp.clip(1.0 + 0.15 * jax.random.normal(seeds[7], (C,), jnp.float32), 0.25, 1.75),
        "w_qkv_col": centred(seeds[8], (C, 3 * C), C ** -0.5, 0.1875, ((0, 16),)),
        "w_out_col": centred(seeds[9], (C, C), C ** -0.5, 0.1875, ((0, 16),)),
    }


def rms_norm(values):
    return values * lax.rsqrt(lax.optimization_barrier(jnp.mean(values * values, axis=-1, keepdims=True)) + 1e-06)

def attend(tokens, w_qkv, w_out):
    batch, length, channels = tokens.shape
    head_dim = channels // HEADS
    projected = jnp.dot(tokens.reshape(-1, channels), w_qkv, preferred_element_type=jnp.float32).astype(jnp.bfloat16)
    projected = projected.reshape(batch, length, 3, HEADS, head_dim).astype(jnp.float32)
    queries = projected[:, :, 0]
    key_heads = projected[:, :, 1]
    values = projected[:, :, 2]
    scores = jnp.einsum('bihd,bjhd->bhij', queries, key_heads) / jnp.sqrt(jnp.float32(head_dim))
    weights_soft = jax.nn.softmax(scores, axis=-1).astype(jnp.bfloat16).astype(jnp.float32)
    mixed = jnp.einsum('bhij,bjhd->bihd', weights_soft, values).astype(jnp.bfloat16)
    outcome = jnp.dot(mixed.reshape(-1, channels), w_out, preferred_element_type=jnp.float32)
    return outcome.reshape(batch, length, channels)

def reference(latents, owners, lead_ids, film_scale, film_shift, w_qkv_row, w_out_row, gain_col, w_qkv_col, w_out_col):
    summed = latents[owners[0]].astype(jnp.float32) + latents[owners[1]].astype(jnp.float32)
    normal_base = rms_norm(summed)

    def one_lead(lead_time):
        hidden = (normal_base * (1.0 + film_scale[lead_time]) + film_shift[lead_time]).astype(jnp.bfloat16)
        after_rows = (hidden.astype(jnp.float32) + attend(hidden, w_qkv_row, w_out_row)).astype(jnp.bfloat16)
        normed = (rms_norm(after_rows.astype(jnp.float32)) * gain_col).astype(jnp.bfloat16)
        column_out = attend(jnp.transpose(normed, (1, 0, 2)), w_qkv_col, w_out_col)
        return (after_rows.astype(jnp.float32) + jnp.transpose(column_out, (1, 0, 2))).astype(jnp.bfloat16)
    return lax.map(one_lead, lead_ids)
```

```python
import functools

import jax
import jax.numpy as jnp
from jax import lax
from jax.experimental import pallas as pl
from jax.experimental.pallas import tpu as pltpu
from jax.sharding import PartitionSpec as P

HEADS = 8
DIM = 128
C = 1024
MESH = pl.DeviceIdType.MESH
BF = jnp.bfloat16
F32 = jnp.float32
TILE = 256
SENDS = 160


def softmax_rows(scores):
    top = jnp.max(scores, axis=-1, keepdims=True)
    weights = jnp.exp((scores - top) * (DIM**-0.5))
    return weights / jnp.sum(weights, axis=-1, keepdims=True)


def kernel(
    slab_in, owners, lead_ids, scale_in, shift_in, wqr_in, wor_in, gain, wqc_in, woc_in,
    out,
    slab, scale_t, shift_t, rx, sx, rz, nb, hid, kv, qb, mixed, send, cols, xf,
    wqr, wor, wqc, woc,
    ssem, loc, s_rx, s_rz, s_ax, s_az, s_wz, s_wy, s_wx, s_wd, s_a2a,
):
    lead = lax.axis_index("lead")
    space = lax.axis_index("space")
    x, zl = lead // 4, lead % 4
    h, y, c = space // 8, (space // 2) % 4, space % 2
    z = h * 4 + zl
    p = x % 2
    yc = space % 8

    def at(x=x, y=y, z=z, c=c):
        return ((x % 4) * 4 + z % 4, (z // 4) * 8 + (y % 4) * 2 + c)

    def zmod(v):
        return (v + 8) % 8

    started = []

    def push(src, dst, recv, dev):
        copy = pltpu.make_async_remote_copy(
            src, dst, ssem.at[len(started)], recv, device_id=dev, device_id_type=MESH
        )
        copy.start()
        started.append(copy)

    def arrived(dst, recv):
        pltpu.make_async_remote_copy(
            dst, dst, ssem.at[0], recv, device_id=at(c=1 - c), device_id_type=MESH
        ).wait_recv()

    weights_in = ((wqr_in, wor_in), (wqc_in, woc_in))
    weights = ((wqr, wor), (wqc, woc))

    local = []

    def pull(src, dst):
        copy = pltpu.make_async_copy(src, dst, loc.at[len(local)])
        copy.start()
        local.append(copy)
        return copy

    slab_copy = pull(slab_in, slab)
    half = pl.ds(pl.multiple_of(p * 32, 32), 32)
    other_half = pl.ds(pl.multiple_of((1 - p) * 32, 32), 32)
    own_copies = [
        [pull(weights_in[a][j].at[half], weights[a][j].at[h, y, c, half]) for j in range(2)]
        for a in range(2)
    ]
    table_copies = [pull(scale_in, scale_t), pull(shift_in, shift_t)]

    barrier = pltpu.get_barrier_semaphore()
    peers = [at(x=x + d) for d in range(1, 4)]
    peers += [at(z=zmod(z + d)) for d in range(1, 8)]
    peers += [at(y=y + d, c=e) for d in range(1, 4) for e in range(2)]
    peers += [at(c=1 - c)]
    for peer in peers:
        pl.semaphore_signal(barrier, 1, device_id=peer, device_id_type=MESH)
    pl.semaphore_wait(barrier, len(peers))

    def weights_z(a):
        for j in range(2):
            push(weights_in[a][j].at[half], weights[a][j].at[h, y, c, half], s_wz.at[a, j], at(z=7 - z))

    def weights_z_arrived(a):
        for j in range(2):
            arrived(weights[a][j].at[1 - h, y, c, half], s_wz.at[a, j])

    def weights_y(a, k):
        for j in range(2):
            hh = h if k == 0 else 1 - h
            block = weights[a][j].at[hh, y, c, half]
            src = weights_in[a][j].at[half] if k == 0 else block
            for d in (1, 3, 2):
                push(src, block, s_wy.at[a, j, k, d - 1], at(y=y + d))

    def weights_x(a, k):
        hh = h if k == 0 else 1 - h
        for j in range(2):
            if k == 0:
                own_copies[a][j].wait()
            for d in (1, 3, 2):
                arrived(weights[a][j].at[hh, (y + 4 - d) % 4, c, half], s_wy.at[a, j, k, d - 1])
            for e in range(2):
                rows = pl.ds(pl.multiple_of(p * 32 + e * 16, 16), 16)
                block = weights[a][j].at[hh, :, c, rows]
                push(block, block, s_wx.at[a, j, k, e], at(x=x + (1 if e == 0 else 3)))
            block = weights[a][j].at[hh, :, c, half]
            push(block, block, s_wd.at[a, j, k, 0], at(c=1 - c))

    def weights_d(a, k):
        hh = h if k == 0 else 1 - h
        for j in range(2):
            for e in range(2):
                rows = pl.ds(pl.multiple_of((1 - p) * 32 + e * 16, 16), 16)
                arrived(weights[a][j].at[hh, :, c, rows], s_wx.at[a, j, k, e])
            block = weights[a][j].at[hh, :, c, other_half]
            push(block, block, s_wd.at[a, j, k, 1], at(c=1 - c))

    def weights_ready(a, j):
        for k in range(2):
            hh = h if k == 0 else 1 - h
            arrived(weights[a][j].at[hh, :, 1 - c, half], s_wd.at[a, j, k, 0])
            arrived(weights[a][j].at[hh, :, 1 - c, other_half], s_wd.at[a, j, k, 1])

    weights_z(0)
    slab_copy.wait()
    mine = jnp.logical_or(owners[0] == lead, owners[1] == lead)
    keep = jnp.where(mine, 1.0, 0.0).astype(F32)

    @pl.loop(0, 8)
    def _(i):
        rows = pl.ds(pl.multiple_of(i * 64, 64), 64)
        slab[rows, :] = (slab[rows, :].astype(F32) * keep).astype(BF)

    for d in (1, 3, 2):
        xt = (x + d) % 4
        push(slab.at[pl.ds(pl.multiple_of(xt * 128, 128), 128)], rx.at[d - 1], s_rx.at[d - 1], at(x=xt))
    weights_y(0, 0)
    for d in (1, 3, 2):
        arrived(rx.at[d - 1], s_rx.at[d - 1])

    @pl.loop(0, 4)
    def _(i):
        rows = pl.ds(pl.multiple_of(i * 32, 32), 32)
        own = slab[pl.ds(pl.multiple_of(x * 128 + i * 32, 32), 32), :].astype(F32)
        total = own + rx[0, rows, :].astype(F32) + rx[1, rows, :].astype(F32) + rx[2, rows, :].astype(F32)
        sx[rows, :] = total.astype(BF)

    for d in (1, 3, 2):
        zt = (zl + d) % 4
        push(sx.at[pl.ds(pl.multiple_of(zt * 32, 32), 32)], rz.at[d - 1], s_rz.at[d - 1], at(z=h * 4 + zt))
    weights_z_arrived(0)
    weights_y(0, 1)
    for d in (1, 3, 2):
        arrived(rz.at[d - 1], s_rz.at[d - 1])
    total = sx[pl.ds(pl.multiple_of(zl * 32, 32), 32), :].astype(F32)
    total = total + rz[0].astype(F32) + rz[1].astype(F32) + rz[2].astype(F32)
    total = total * lax.rsqrt(jnp.mean(total * total, axis=-1, keepdims=True) + 1e-06)
    nb[h, x, zl] = total.astype(BF)

    for d in (1, 3, 2):
        piece = nb.at[h, x, zl]
        push(piece, piece, s_ax.at[d - 1], at(x=x + d))
    for d in (1, 3, 2):
        arrived(nb.at[h, (x + 4 - d) % 4, zl], s_ax.at[d - 1])

    def ring_rows(t, way):
        return slice(0, 4) if t < 4 else (slice(0, 2) if way == 0 else slice(2, 4))

    def ring_send(t):
        for way in range(2):
            source = zmod(z - (t - 1)) if way == 0 else zmod(z + (t - 1))
            target = zmod(z + 1) if way == 0 else zmod(z - 1)
            rows = ring_rows(t, way)
            piece = nb.at[source // 4, pl.ds(rows.start, rows.stop - rows.start), source % 4]
            push(piece, piece, s_az.at[t - 1, way], at(z=target))

    def ring_arrived(t):
        for way in range(2):
            source = zmod(z - t) if way == 0 else zmod(z + t)
            rows = ring_rows(t, way)
            arrived(
                nb.at[source // 4, pl.ds(rows.start, rows.stop - rows.start), source % 4],
                s_az.at[t - 1, way],
            )

    ring_send(1)
    weights_x(0, 0)
    ring_arrived(1)
    ring_send(2)
    weights_x(0, 1)
    weights_z(1)
    weights_y(1, 0)
    ring_arrived(2)
    ring_send(3)
    weights_d(0, 0)
    ring_arrived(3)
    ring_send(4)
    weights_d(0, 1)
    weights_z_arrived(1)
    weights_y(1, 1)
    for copy in table_copies:
        copy.wait()
    time = lead_ids[0]
    film_gain = 1.0 + scale_t[pl.ds(time, 1), :]
    film_bias = shift_t[pl.ds(time, 1), :]
    ring_arrived(4)
    weights_ready(0, 0)

    def row_step(hp):
        @pl.loop(0, 8)
        def _(i):
            part = nb[hp, i // 2, pl.ds((i % 2) * 2, 2)].reshape(64, C)
            rows = pl.ds(pl.multiple_of(i * 64, 64), 64)
            hid[rows, :] = (part.astype(F32) * film_gain + film_bias).astype(BF)

        @pl.loop(0, 8)
        def _(t):
            block = wqr[:, :, :, :, pl.ds(pl.multiple_of(C + t * TILE, TILE), TILE)].reshape(C, TILE)
            cut = pl.ds(pl.multiple_of(t * TILE, TILE), TILE)
            kv[:, cut] = jnp.dot(hid[...], block, preferred_element_type=F32).astype(BF)

        here = pl.ds(pl.multiple_of(h * 64, 64), 64)

        def wanted(cols_cut):
            return jnp.concatenate(
                [hid[pl.ds(pl.multiple_of(r * 128 + h * 64, 64), 64), cols_cut] for r in range(4)], axis=0
            )

        @pl.loop(0, 4)
        def _(t):
            cut = pl.ds(pl.multiple_of(t * TILE, TILE), TILE)
            block = wqr[:, :, :, :, cut].reshape(C, TILE)
            qb[:, cut] = jnp.dot(wanted(slice(None)), block, preferred_element_type=F32).astype(BF)

        for head in range(HEADS):
            cut = slice(head * DIM, (head + 1) * DIM)
            vcut = slice(C + head * DIM, C + (head + 1) * DIM)
            q = qb[:, cut].reshape(4, 64, DIM)
            keys = kv[:, cut].reshape(4, 128, DIM)
            values = kv[:, vcut].reshape(4, 128, DIM)
            scores = lax.dot_general(q, keys, (((2,), (2,)), ((0,), (0,))), preferred_element_type=F32)
            probs = softmax_rows(scores).astype(BF)
            mix = lax.dot_general(probs, values, (((2,), (1,)), ((0,), (0,))), preferred_element_type=F32)
            mixed[pl.ds(0, 256), cut] = mix.reshape(256, DIM).astype(BF)

        if hp == 0:
            weights_ready(0, 1)

        @pl.loop(0, 4)
        def _(t):
            cut = pl.ds(pl.multiple_of(t * TILE, TILE), TILE)
            block = wor[:, :, :, :, cut].reshape(C, TILE)
            grown = jnp.dot(mixed[pl.ds(0, 256), :], block, preferred_element_type=F32)
            grown = (grown + wanted(cut).astype(F32)).reshape(4, 64, TILE)
            for d in range(8):
                send[hp, d, :, cut] = grown[:, d * 8 : (d + 1) * 8, :].reshape(32, TILE).astype(BF)

        for dy in (2, 1, 3, 0):
            for dc in range(2):
                if dy == 0 and dc == 0:
                    continue
                ty, tc = (y + dy) % 4, (c + dc) % 2
                push(
                    send.at[hp, ty * 2 + tc], cols.at[hp, yc], s_a2a.at[hp, dy * 2 + dc], at(y=ty, c=tc)
                )
        return pull(send.at[hp, yc], cols.at[hp, yc])

    def row_arrived(hp):
        for dy in (2, 1, 3, 0):
            for dc in range(2):
                if dy == 0 and dc == 0:
                    continue
                sy, sc = (y + 4 - dy) % 4, (c + dc) % 2
                arrived(cols.at[hp, sy * 2 + sc], s_a2a.at[hp, dy * 2 + dc])

    own0 = row_step(0)
    weights_x(1, 0)
    own1 = row_step(1)
    weights_x(1, 1)
    weights_d(1, 0)
    weights_d(1, 1)
    own0.wait()
    own1.wait()
    row_arrived(0)
    row_arrived(1)

    for hp in range(2):
        @pl.loop(0, 8)
        def _(i):
            part = cols[hp, i].astype(F32)
            part = part * lax.rsqrt(jnp.mean(part * part, axis=-1, keepdims=True) + 1e-06) * gain[...]
            rows = pl.ds(pl.multiple_of(hp * 256 + i * 32, 32), 32)
            for s in range(8):
                xf[s, rows, :] = part[:, s * DIM : (s + 1) * DIM]

    for w in range(8):
        for s in range(8):
            hid[w * 64 : (w + 1) * 64, s * DIM : (s + 1) * DIM] = xf[s, pl.ds(w, 64, stride=8), :].astype(BF)

    weights_ready(1, 0)

    @pl.loop(0, 8)
    def _(t):
        block = wqc[:, :, :, :, pl.ds(pl.multiple_of(C + t * TILE, TILE), TILE)].reshape(C, TILE)
        cut = pl.ds(pl.multiple_of(t * TILE, TILE), TILE)
        kv[:, cut] = jnp.dot(hid[...], block, preferred_element_type=F32).astype(BF)

    @pl.loop(0, 4)
    def _(t):
        cut = pl.ds(pl.multiple_of(t * TILE, TILE), TILE)
        block = wqc[:, :, :, :, cut].reshape(C, TILE)
        mixed[:, cut] = jnp.dot(hid[...], block, preferred_element_type=F32).astype(BF)

    for head in range(HEADS):
        cut = slice(head * DIM, (head + 1) * DIM)
        vcut = slice(C + head * DIM, C + (head + 1) * DIM)
        q = mixed[:, cut].reshape(8, 64, DIM)
        keys = kv[:, cut].reshape(8, 64, DIM)
        values = kv[:, vcut].reshape(8, 64, DIM)
        scores = lax.dot_general(q, keys, (((2,), (2,)), ((0,), (0,))), preferred_element_type=F32)
        probs = softmax_rows(scores).astype(BF)
        mix = lax.dot_general(probs, values, (((2,), (1,)), ((0,), (0,))), preferred_element_type=F32)
        for w in range(8):
            xf[head, pl.ds(w, 64, stride=8), :] = mix[w]
        hid[:, cut] = xf[head].astype(BF)

    weights_ready(1, 1)

    @pl.loop(0, 4)
    def _(t):
        cut = pl.ds(pl.multiple_of(t * TILE, TILE), TILE)
        block = woc[:, :, :, :, cut].reshape(C, TILE)
        grown = jnp.dot(hid[...], block, preferred_element_type=F32)
        out[:, cut] = (grown + cols[:, :, :, cut].reshape(512, TILE).astype(F32)).astype(BF)

    for copy in started:
        copy.wait_send()


def on_device(
    latents, owners, lead_ids, film_scale, film_shift, w_qkv_row, w_out_row, gain_col, w_qkv_col, w_out_col
):
    anywhere = pl.BlockSpec(memory_space=pl.ANY)
    scalars = pl.BlockSpec(memory_space=pltpu.SMEM)
    vector = pl.BlockSpec(memory_space=pltpu.VMEM)
    dma = pltpu.SemaphoreType.DMA
    result = pl.pallas_call(
        kernel,
        out_shape=jax.ShapeDtypeStruct((512, C), BF),
        in_specs=[
            anywhere, scalars, scalars, anywhere, anywhere, anywhere, anywhere, vector, anywhere, anywhere
        ],
        out_specs=vector,
        scratch_shapes=[
            pltpu.VMEM((512, C), BF),
            pltpu.VMEM((360, C), F32),
            pltpu.VMEM((360, C), F32),
            pltpu.VMEM((3, 128, C), BF),
            pltpu.VMEM((128, C), BF),
            pltpu.VMEM((3, 32, C), BF),
            pltpu.VMEM((2, 4, 4, 32, C), BF),
            pltpu.VMEM((512, C), BF),
            pltpu.VMEM((512, 2 * C), BF),
            pltpu.VMEM((256, C), BF),
            pltpu.VMEM((512, C), BF),
            pltpu.VMEM((2, 8, 32, C), BF),
            pltpu.VMEM((2, 8, 32, C), BF),
            pltpu.VMEM((8, 512, DIM), F32),
            pltpu.VMEM((2, 4, 2, 64, 3 * C), BF),
            pltpu.VMEM((2, 4, 2, 64, C), BF),
            pltpu.VMEM((2, 4, 2, 64, 3 * C), BF),
            pltpu.VMEM((2, 4, 2, 64, C), BF),
            dma((SENDS,)),
            dma((9,)),
            dma((3,)),
            dma((3,)),
            dma((3,)),
            dma((4, 2)),
            dma((2, 2)),
            dma((2, 2, 2, 3)),
            dma((2, 2, 2, 2)),
            dma((2, 2, 2, 2)),
            dma((2, 8)),
        ],
        compiler_params=pltpu.CompilerParams(
            collective_id=0, has_side_effects=True, vmem_limit_bytes=56 << 20
        ),
        name="axial_attention",
    )(
        latents.reshape(512, C), owners, lead_ids, film_scale, film_shift,
        w_qkv_row, w_out_row, gain_col.reshape(1, C), w_qkv_col, w_out_col,
    )
    return result.reshape(1, 64, 8, C)


def solution(mesh):
    placed = (
        P("lead", "space", None, None),
        P(),
        P("lead"),
        P(),
        P(),
        P("space", None),
        P("space", None),
        P(),
        P("space", None),
        P("space", None),
    )
    return jax.shard_map(
        on_device,
        mesh=mesh,
        in_specs=placed,
        out_specs=P("lead", None, "space", None),
        check_vma=False,
    )
```

```python
import functools

import jax
import jax.numpy as jnp
from jax import lax
from jax.experimental import pallas as pl
from jax.experimental.pallas import tpu as pltpu
from jax.sharding import PartitionSpec as P

HEADS = 8
DIM = 128
C = 1024
MESH = pl.DeviceIdType.MESH
BF = jnp.bfloat16
F32 = jnp.float32
TILE = 1024
SENDS = 200


def softmax_rows(scores):
    top = jnp.max(scores, axis=-1, keepdims=True)
    weights = jnp.exp((scores - top) * (DIM**-0.5))
    return weights / jnp.sum(weights, axis=-1, keepdims=True)


def kernel(
    slab_in, owners, lead_ids, scale_in, shift_in, wqr_in, wor_in, gain, wqc_in, woc_in,
    out,
    slab, scale_t, shift_t, rx, sx, rz, nb, hid, kv, qb, mixed, send, cols, xf,
    wqr, wor, wqc, woc,
    ssem, loc, s_rx, s_rz, s_ax, s_az, s_edge, s_ny, s_wz, s_wy, s_wf, s_wx, s_wd, s_a2a,
):
    lead = lax.axis_index("lead")
    space = lax.axis_index("space")
    x, zl = lead // 4, lead % 4
    h, y, c = space // 8, (space // 2) % 4, space % 2
    z = h * 4 + zl
    p = x % 2
    yc = space % 8

    def at(x=x, y=y, z=z, c=c):
        return ((x % 4) * 4 + z % 4, (z // 4) * 8 + (y % 4) * 2 + c)

    def zmod(v):
        return (v + 8) % 8

    started = []

    def push(src, dst, recv, dev):
        copy = pltpu.make_async_remote_copy(
            src, dst, ssem.at[len(started)], recv, device_id=dev, device_id_type=MESH
        )
        copy.start()
        started.append(copy)

    def arrived(dst, recv):
        pltpu.make_async_remote_copy(
            dst, dst, ssem.at[0], recv, device_id=at(c=1 - c), device_id_type=MESH
        ).wait_recv()

    weights_in = ((wqr_in, wor_in), (wqc_in, woc_in))
    weights = ((wqr, wor), (wqc, woc))

    local = []

    def pull(src, dst):
        copy = pltpu.make_async_copy(src, dst, loc.at[len(local)])
        copy.start()
        local.append(copy)
        return copy

    slab_copy = pull(slab_in, slab)
    half = pl.ds(pl.multiple_of(p * 32, 32), 32)
    other_half = pl.ds(pl.multiple_of((1 - p) * 32, 32), 32)
    own_copies = [
        [pull(weights_in[0][j].at[half], weights[0][j].at[h, y, c, half]) for j in range(2)],
        [pull(weights_in[1][j], weights[1][j].at[h, y, c]) for j in range(2)],
    ]
    table_copies = [pull(scale_in, scale_t), pull(shift_in, shift_t)]

    barrier = pltpu.get_barrier_semaphore()
    peers = [at(x=x + d) for d in range(1, 4)]
    peers += [at(y=y + d) for d in range(1, 4)]
    peers += [at(z=h * 4 + (zl + d) % 4) for d in range(1, 4)]
    peers += [at(z=7 - z), at(c=1 - c)]
    for peer in peers:
        pl.semaphore_signal(barrier, 1, device_id=peer, device_id_type=MESH)
    pl.semaphore_wait(barrier, len(peers))

    def side(k):
        return h if k == 0 else 1 - h

    edge = jnp.logical_or(zl == 0, zl == 3)
    inner = h * 4 + jnp.where(zl == 0, 1, 2)

    def edge_copy(a, j, forward):
        own = weights_in[a][j].at[half]
        there = weights[a][j].at[h, y, c, half]
        far = weights[a][j].at[1 - h, y, c, half]
        return pltpu.make_async_remote_copy(
            far if forward else own,
            far if forward else there,
            s_edge.at[a, j, int(forward)],
            s_wz.at[a, j],
            device_id=at(z=inner if forward else 7 - z),
            device_id_type=MESH,
        )

    def far_z(a, j):
        @pl.when(edge)
        def _():
            edge_copy(a, j, False).start()

    def far_y(a, j, k):
        block = weights[a][j].at[side(k), y, c, half]
        if k == 1:
            arrived(block, s_wz.at[a, j])

            @pl.when(edge)
            def _():
                edge_copy(a, j, True).start()

        src = weights_in[a][j].at[half] if k == 0 else block
        for d in (1, 3):
            push(src, block, s_wy.at[a, j, k, d // 2], at(y=y + d))

    def quarter(parity, e):
        return pl.ds(pl.multiple_of(parity * 32 + e * 16, 16), 16)

    def far_push(a, j, k, d):
        for e in range(2):
            block = weights[a][j].at[side(k), (y + d) % 4, c, quarter(p, e)]
            push(block, block, s_wx.at[a, j, k, e, d], at(x=x + (1 if e == 0 else 3)))

    def far_f(a, j, k):
        for e in range(2):
            d = 1 if e == 0 else 3
            near = weights[a][j].at[side(k), (y + 4 - d) % 4, c]
            arrived(near.at[half], s_wy.at[a, j, k, e])
            push(near.at[quarter(p, e)], near.at[quarter(p, e)], s_wf.at[a, j, k, e], at(y=y + d))
        if k == 1:
            far_push(a, j, k, 0)
        far_push(a, j, k, 3)
        far_push(a, j, k, 1)

    def far_x(a, j, k):
        for e in range(2):
            arrived(weights[a][j].at[side(k), (y + 2) % 4, c, quarter(p, e)], s_wf.at[a, j, k, e])
        far_push(a, j, k, 2)
        if k == 0:
            own_copies[a][j].wait()
        block = weights[a][j].at[side(k), :, c, half]
        push(block, block, s_wd.at[a, j, k, 0], at(c=1 - c))

    def far_d(a, j, k):
        for d in ((3, 1, 2) if k == 0 else (0, 3, 1, 2)):
            for e in range(2):
                arrived(weights[a][j].at[side(k), (y + d) % 4, c, quarter(1 - p, e)], s_wx.at[a, j, k, e, d])
        block = weights[a][j].at[side(k), :, c, other_half]
        push(block, block, s_wd.at[a, j, k, 1], at(c=1 - c))

    def near_z(j):
        push(weights_in[0][j].at[half], weights[0][j].at[h, y, c, half], s_wz.at[0, j], at(z=7 - z))

    def near_y(j, k):
        block = weights[0][j].at[side(k), y, c, half]
        if k == 1:
            arrived(block, s_wz.at[0, j])
        src = weights_in[0][j].at[half] if k == 0 else block
        for d in (1, 3, 2):
            push(src, block, s_ny.at[j, k, d - 1], at(y=y + d))

    def near_x(j, k):
        if k == 0:
            own_copies[0][j].wait()
        for d in (1, 3, 2):
            arrived(weights[0][j].at[side(k), (y + 4 - d) % 4, c, half], s_ny.at[j, k, d - 1])
        for e in range(2):
            block = weights[0][j].at[side(k), :, c, quarter(p, e)]
            push(block, block, s_wx.at[0, j, k, e, 0], at(x=x + (1 if e == 0 else 3)))
        block = weights[0][j].at[side(k), :, c, half]
        push(block, block, s_wd.at[0, j, k, 0], at(c=1 - c))

    def near_d(j, k):
        for e in range(2):
            arrived(weights[0][j].at[side(k), :, c, quarter(1 - p, e)], s_wx.at[0, j, k, e, 0])
        block = weights[0][j].at[side(k), :, c, other_half]
        push(block, block, s_wd.at[0, j, k, 1], at(c=1 - c))

    def weights_ready(a, j):
        for k in range(2):
            arrived(weights[a][j].at[side(k), :, 1 - c, half], s_wd.at[a, j, k, 0])
            arrived(weights[a][j].at[side(k), :, 1 - c, other_half], s_wd.at[a, j, k, 1])

    mine = jnp.logical_or(owners[0] == lead, owners[1] == lead)
    keep = jnp.where(mine, 1.0, 0.0).astype(F32)

    def reduce_x(b):
        for d in (1, 3, 2):
            xt = (x + d) % 4
            push(slab.at[xt, :, b], rx.at[d - 1, :, b], s_rx.at[b, d - 1], at(x=xt))

    def reduce_x_arrived(b):
        for d in (1, 3, 2):
            arrived(rx.at[d - 1, :, b], s_rx.at[b, d - 1])

    def reduce_z(b):
        for i in range(4):
            total = slab[x, i, b].astype(F32) + rx[0, i, b].astype(F32)
            total = total + rx[1, i, b].astype(F32) + rx[2, i, b].astype(F32)
            sx[i, b] = total.astype(BF)
        for d in (1, 3, 2):
            zt = (zl + d) % 4
            push(sx.at[zt, b], rz.at[d - 1, b], s_rz.at[b, d - 1], at(z=h * 4 + zt))

    def gather_x(b):
        for d in (1, 3, 2):
            arrived(rz.at[d - 1, b], s_rz.at[b, d - 1])
        total = sx[zl, b].astype(F32) + rz[0, b].astype(F32) + rz[1, b].astype(F32) + rz[2, b].astype(F32)
        total = total * lax.rsqrt(jnp.mean(total * total, axis=-1, keepdims=True) + 1e-06)
        nb[h, x, zl, b] = total.astype(BF)
        piece = nb.at[h, x, zl, b]
        for d in (1, 3, 2):
            push(piece, piece, s_ax.at[b, d - 1], at(x=x + d))

    def gather_x_arrived(b):
        for d in (1, 3, 2):
            arrived(nb.at[h, (x + 4 - d) % 4, zl, b], s_ax.at[b, d - 1])

    def ring_piece(source, t, way, b):
        rows = pl.ds(0, 4) if t < 4 else pl.ds(2 * way, 2)
        return nb.at[source // 4, rows, source % 4, b]

    def ring_send(t, b):
        for way in range(2):
            source = zmod(z - (t - 1)) if way == 0 else zmod(z + (t - 1))
            target = zmod(z + 1) if way == 0 else zmod(z - 1)
            piece = ring_piece(source, t, way, b)
            push(piece, piece, s_az.at[b, t - 1, way], at(z=target))

    def ring_arrived(t, b):
        for way in range(2):
            source = zmod(z - t) if way == 0 else zmod(z + t)
            arrived(ring_piece(source, t, way, b), s_az.at[b, t - 1, way])

    near_z(0)
    near_y(0, 0)
    slab_copy.wait()

    @pl.loop(0, 16)
    def _(i):
        slab[i // 4, i % 4] = (slab[i // 4, i % 4].astype(F32) * keep).astype(BF)

    reduce_x(0)
    near_z(1)
    reduce_x_arrived(0)
    reduce_x(1)
    reduce_z(0)
    near_y(0, 1)
    gather_x(0)
    near_y(1, 0)
    near_x(0, 0)
    reduce_x_arrived(1)
    reduce_z(1)
    gather_x_arrived(0)
    ring_send(1, 0)
    gather_x(1)
    near_x(0, 1)
    near_y(1, 1)
    ring_arrived(1, 0)
    ring_send(2, 0)
    gather_x_arrived(1)
    ring_send(1, 1)
    near_x(1, 0)
    far_y(1, 0, 0)
    far_z(1, 0)
    ring_arrived(2, 0)
    ring_send(3, 0)
    ring_arrived(1, 1)
    ring_send(2, 1)
    near_x(1, 1)
    near_d(0, 0)
    ring_arrived(3, 0)
    ring_send(4, 0)
    ring_arrived(2, 1)
    ring_send(3, 1)
    near_d(0, 1)
    far_f(1, 0, 0)
    far_z(1, 1)
    far_y(1, 1, 0)
    ring_arrived(4, 0)
    ring_arrived(3, 1)
    ring_send(4, 1)
    near_d(1, 0)
    near_d(1, 1)
    far_x(1, 0, 0)
    far_y(1, 0, 1)
    far_f(1, 1, 0)
    far_y(1, 1, 1)
    for copy in table_copies:
        copy.wait()
    time = lead_ids[0]
    film_gain = 1.0 + scale_t[pl.ds(time, 1), :]
    film_bias = shift_t[pl.ds(time, 1), :]
    ring_arrived(4, 1)
    weights_ready(0, 0)

    def row_step(hp, first, second):
        @pl.loop(0, 8)
        def _(i):
            part = nb[hp, i // 2, pl.ds((i % 2) * 2, 2)].reshape(64, C)
            rows = pl.ds(pl.multiple_of(i * 64, 64), 64)
            hid[rows, :] = (part.astype(F32) * film_gain + film_bias).astype(BF)

        @pl.loop(0, 2)
        def _(t):
            block = wqr[:, :, :, :, pl.ds(pl.multiple_of(C + t * TILE, TILE), TILE)].reshape(C, TILE)
            cut = pl.ds(pl.multiple_of(t * TILE, TILE), TILE)
            kv[:, cut] = jnp.dot(hid[...], block, preferred_element_type=F32).astype(BF)

        here = pl.ds(pl.multiple_of(h * 64, 64), 64)

        def wanted(cols_cut):
            return jnp.concatenate(
                [hid[pl.ds(pl.multiple_of(r * 128 + h * 64, 64), 64), cols_cut] for r in range(4)], axis=0
            )

        @pl.loop(0, 1)
        def _(t):
            cut = pl.ds(pl.multiple_of(t * TILE, TILE), TILE)
            block = wqr[:, :, :, :, cut].reshape(C, TILE)
            qb[:, cut] = jnp.dot(wanted(slice(None)), block, preferred_element_type=F32).astype(BF)

        first()

        for head in range(HEADS):
            cut = slice(head * DIM, (head + 1) * DIM)
            vcut = slice(C + head * DIM, C + (head + 1) * DIM)
            q = qb[:, cut].reshape(4, 64, DIM)
            keys = kv[:, cut].reshape(4, 128, DIM)
            values = kv[:, vcut].reshape(4, 128, DIM)
            scores = lax.dot_general(q, keys, (((2,), (2,)), ((0,), (0,))), preferred_element_type=F32)
            probs = softmax_rows(scores).astype(BF)
            mix = lax.dot_general(probs, values, (((2,), (1,)), ((0,), (0,))), preferred_element_type=F32)
            mixed[pl.ds(0, 256), cut] = mix.reshape(256, DIM).astype(BF)

        second()

        @pl.loop(0, 1)
        def _(t):
            cut = pl.ds(pl.multiple_of(t * TILE, TILE), TILE)
            block = wor[:, :, :, :, cut].reshape(C, TILE)
            grown = jnp.dot(mixed[pl.ds(0, 256), :], block, preferred_element_type=F32)
            grown = (grown + wanted(cut).astype(F32)).reshape(4, 64, TILE)
            for d in range(8):
                send[hp, d, :, cut] = grown[:, d * 8 : (d + 1) * 8, :].reshape(32, TILE).astype(BF)

        for dy in (2, 1, 3, 0):
            for dc in range(2):
                if dy == 0 and dc == 0:
                    continue
                ty, tc = (y + dy) % 4, (c + dc) % 2
                push(
                    send.at[hp, ty * 2 + tc], cols.at[hp, yc], s_a2a.at[hp, dy * 2 + dc], at(y=ty, c=tc)
                )
        return pull(send.at[hp, yc], cols.at[hp, yc])

    def row_arrived(hp):
        for dy in (2, 1, 3, 0):
            for dc in range(2):
                if dy == 0 and dc == 0:
                    continue
                sy, sc = (y + 4 - dy) % 4, (c + dc) % 2
                arrived(cols.at[hp, sy * 2 + sc], s_a2a.at[hp, dy * 2 + dc])

    def after_first_projection():
        far_f(1, 0, 1)
        far_x(1, 1, 0)
        far_d(1, 0, 0)

    def after_first_mix():
        far_f(1, 1, 1)
        far_x(1, 0, 1)
        weights_ready(0, 1)

    def after_second_projection():
        far_x(1, 1, 1)
        far_d(1, 1, 0)
        far_d(1, 0, 1)

    def after_second_mix():
        far_d(1, 1, 1)

    own0 = row_step(0, after_first_projection, after_first_mix)
    own1 = row_step(1, after_second_projection, after_second_mix)
    own0.wait()
    own1.wait()
    row_arrived(0)
    row_arrived(1)

    for hp in range(2):
        @pl.loop(0, 8)
        def _(i):
            part = cols[hp, i].astype(F32)
            part = part * lax.rsqrt(jnp.mean(part * part, axis=-1, keepdims=True) + 1e-06) * gain[...]
            rows = pl.ds(pl.multiple_of(hp * 256 + i * 32, 32), 32)
            for s in range(8):
                xf[s, rows, :] = part[:, s * DIM : (s + 1) * DIM]

    for w in range(8):
        for s in range(8):
            hid[w * 64 : (w + 1) * 64, s * DIM : (s + 1) * DIM] = xf[s, pl.ds(w, 64, stride=8), :].astype(BF)

    weights_ready(1, 0)

    @pl.loop(0, 2)
    def _(t):
        block = wqc[:, :, :, :, pl.ds(pl.multiple_of(C + t * TILE, TILE), TILE)].reshape(C, TILE)
        cut = pl.ds(pl.multiple_of(t * TILE, TILE), TILE)
        kv[:, cut] = jnp.dot(hid[...], block, preferred_element_type=F32).astype(BF)

    @pl.loop(0, 1)
    def _(t):
        cut = pl.ds(pl.multiple_of(t * TILE, TILE), TILE)
        block = wqc[:, :, :, :, cut].reshape(C, TILE)
        mixed[:, cut] = jnp.dot(hid[...], block, preferred_element_type=F32).astype(BF)

    for head in range(HEADS):
        cut = slice(head * DIM, (head + 1) * DIM)
        vcut = slice(C + head * DIM, C + (head + 1) * DIM)
        q = mixed[:, cut].reshape(8, 64, DIM)
        keys = kv[:, cut].reshape(8, 64, DIM)
        values = kv[:, vcut].reshape(8, 64, DIM)
        scores = lax.dot_general(q, keys, (((2,), (2,)), ((0,), (0,))), preferred_element_type=F32)
        probs = softmax_rows(scores).astype(BF)
        mix = lax.dot_general(probs, values, (((2,), (1,)), ((0,), (0,))), preferred_element_type=F32)
        for w in range(8):
            xf[head, pl.ds(w, 64, stride=8), :] = mix[w]
        hid[:, cut] = xf[head].astype(BF)

    weights_ready(1, 1)

    @pl.loop(0, 1)
    def _(t):
        cut = pl.ds(pl.multiple_of(t * TILE, TILE), TILE)
        block = woc[:, :, :, :, cut].reshape(C, TILE)
        grown = jnp.dot(hid[...], block, preferred_element_type=F32)
        out[:, cut] = (grown + cols[:, :, :, cut].reshape(512, TILE).astype(F32)).astype(BF)

    for copy in started:
        copy.wait_send()

    @pl.when(edge)
    def _():
        for a in range(1, 2):
            for j in range(2):
                for forward in (False, True):
                    edge_copy(a, j, forward).wait_send()


def on_device(
    latents, owners, lead_ids, film_scale, film_shift, w_qkv_row, w_out_row, gain_col, w_qkv_col, w_out_col
):
    anywhere = pl.BlockSpec(memory_space=pl.ANY)
    scalars = pl.BlockSpec(memory_space=pltpu.SMEM)
    vector = pl.BlockSpec(memory_space=pltpu.VMEM)
    dma = pltpu.SemaphoreType.DMA
    result = pl.pallas_call(
        kernel,
        out_shape=jax.ShapeDtypeStruct((512, C), BF),
        in_specs=[
            anywhere, scalars, scalars, anywhere, anywhere, anywhere, anywhere, vector, anywhere, anywhere
        ],
        out_specs=vector,
        scratch_shapes=[
            pltpu.VMEM((4, 4, 2, 16, C), BF),
            pltpu.VMEM((360, C), F32),
            pltpu.VMEM((360, C), F32),
            pltpu.VMEM((3, 4, 2, 16, C), BF),
            pltpu.VMEM((4, 2, 16, C), BF),
            pltpu.VMEM((3, 2, 16, C), BF),
            pltpu.VMEM((2, 4, 4, 2, 16, C), BF),
            pltpu.VMEM((512, C), BF),
            pltpu.VMEM((512, 2 * C), BF),
            pltpu.VMEM((256, C), BF),
            pltpu.VMEM((512, C), BF),
            pltpu.VMEM((2, 8, 32, C), BF),
            pltpu.VMEM((2, 8, 32, C), BF),
            pltpu.VMEM((8, 512, DIM), F32),
            pltpu.VMEM((2, 4, 2, 64, 3 * C), BF),
            pltpu.VMEM((2, 4, 2, 64, C), BF),
            pltpu.VMEM((2, 4, 2, 64, 3 * C), BF),
            pltpu.VMEM((2, 4, 2, 64, C), BF),
            dma((SENDS,)),
            dma((9,)),
            dma((2, 3)),
            dma((2, 3)),
            dma((2, 3)),
            dma((2, 4, 2)),
            dma((2, 2, 2)),
            dma((2, 2, 3)),
            dma((2, 2)),
            dma((2, 2, 2, 2)),
            dma((2, 2, 2, 2)),
            dma((2, 2, 2, 2, 4)),
            dma((2, 2, 2, 2)),
            dma((2, 8)),
        ],
        compiler_params=pltpu.CompilerParams(
            collective_id=0, has_side_effects=True, vmem_limit_bytes=56 << 20
        ),
        name="axial_attention",
    )(
        latents.reshape(4, 4, 2, 16, C), owners, lead_ids, film_scale, film_shift,
        w_qkv_row, w_out_row, gain_col.reshape(1, C), w_qkv_col, w_out_col,
    )
    return result.reshape(1, 64, 8, C)


def solution(mesh):
    placed = (
        P("lead", "space", None, None),
        P(),
        P("lead"),
        P(),
        P(),
        P("space", None),
        P("space", None),
        P(),
        P("space", None),
        P("space", None),
    )
    return jax.shard_map(
        on_device,
        mesh=mesh,
        in_specs=placed,
        out_specs=P("lead", None, "space", None),
        check_vma=False,
    )
```

```python
import functools

import jax
import jax.numpy as jnp
from jax import lax
from jax.experimental import pallas as pl
from jax.experimental.pallas import tpu as pltpu
from jax.sharding import PartitionSpec as P

HEADS = 8
DIM = 128
C = 1024
MESH = pl.DeviceIdType.MESH
BF = jnp.bfloat16
F32 = jnp.float32
TILE = 1024
SENDS = 200


def attend(q, keys, values):
    batch, count, _ = q.shape
    scores = lax.dot_general(q, keys, (((2,), (2,)), ((0,), (0,))), preferred_element_type=F32)
    top = jnp.max(scores, axis=-1, keepdims=True)
    weights = jnp.exp((scores - top) * (DIM**-0.5)).astype(BF)
    mix = lax.dot_general(weights, values, (((2,), (1,)), ((0,), (0,))), preferred_element_type=F32)
    ones = jnp.ones((keys.shape[1], DIM), BF)
    total = jnp.dot(weights.reshape(batch * count, keys.shape[1]), ones, preferred_element_type=F32)
    return mix.reshape(batch * count, DIM) / total


def kernel(
    slab_in, owners, lead_ids, scale_in, shift_in, wqr_in, wor_in, gain, wqc_in, woc_in,
    out,
    slab, scale_t, shift_t, rx, sx, rz, nb, hid, xt, kv, kvc, qb, mixed, send, cols, xf,
    wqr, wor, wqc, woc,
    ssem, loc, s_rx, s_rz, s_ax, s_az, s_edge, s_ny, s_wz, s_wy, s_wf, s_wx, s_wd, s_a2a,
):
    lead = lax.axis_index("lead")
    space = lax.axis_index("space")
    x, zl = lead // 4, lead % 4
    h, y, c = space // 8, (space // 2) % 4, space % 2
    z = h * 4 + zl
    p = x % 2
    yc = space % 8

    def at(x=x, y=y, z=z, c=c):
        return ((x % 4) * 4 + z % 4, (z // 4) * 8 + (y % 4) * 2 + c)

    def zmod(v):
        return (v + 8) % 8

    started = []

    def push(src, dst, recv, dev):
        copy = pltpu.make_async_remote_copy(
            src, dst, ssem.at[len(started)], recv, device_id=dev, device_id_type=MESH
        )
        copy.start()
        started.append(copy)

    def arrived(dst, recv):
        pltpu.make_async_remote_copy(
            dst, dst, ssem.at[0], recv, device_id=at(c=1 - c), device_id_type=MESH
        ).wait_recv()

    weights_in = ((wqr_in, wor_in), (wqc_in, woc_in))
    weights = ((wqr, wor), (wqc, woc))

    local = []

    def pull(src, dst):
        copy = pltpu.make_async_copy(src, dst, loc.at[len(local)])
        copy.start()
        local.append(copy)
        return copy

    slab_copy = pull(slab_in, slab)
    half = pl.ds(pl.multiple_of(p * 32, 32), 32)
    other_half = pl.ds(pl.multiple_of((1 - p) * 32, 32), 32)
    own_copies = [
        [pull(weights_in[0][j].at[half], weights[0][j].at[h, y, c, half]) for j in range(2)],
        [pull(weights_in[1][j], weights[1][j].at[h, y, c]) for j in range(2)],
    ]
    table_copies = [pull(scale_in, scale_t), pull(shift_in, shift_t)]

    barrier = pltpu.get_barrier_semaphore()
    peers = [at(x=x + d) for d in range(1, 4)]
    peers += [at(y=y + d) for d in range(1, 4)]
    peers += [at(z=h * 4 + (zl + d) % 4) for d in range(1, 4)]
    peers += [at(z=7 - z), at(c=1 - c)]
    for peer in peers:
        pl.semaphore_signal(barrier, 1, device_id=peer, device_id_type=MESH)
    mine = jnp.logical_or(owners[0] == lead, owners[1] == lead)
    keep = jnp.where(mine, 1.0, 0.0).astype(F32)
    slab_copy.wait()

    @pl.loop(0, 16)
    def _(i):
        slab[i // 4, i % 4] = (slab[i // 4, i % 4].astype(F32) * keep).astype(BF)

    pl.semaphore_wait(barrier, len(peers))

    def side(k):
        return h if k == 0 else 1 - h

    edge = jnp.logical_or(zl == 0, zl == 3)
    inner = h * 4 + jnp.where(zl == 0, 1, 2)

    def edge_copy(a, j, forward):
        own = weights_in[a][j].at[half]
        there = weights[a][j].at[h, y, c, half]
        far = weights[a][j].at[1 - h, y, c, half]
        return pltpu.make_async_remote_copy(
            far if forward else own,
            far if forward else there,
            s_edge.at[a, j, int(forward)],
            s_wz.at[a, j],
            device_id=at(z=inner if forward else 7 - z),
            device_id_type=MESH,
        )

    def mirror_send(a, j):
        @pl.when(edge)
        def _():
            edge_copy(a, j, False).start()

    def mirror_pass(a, j):
        @pl.when(edge)
        def _():
            arrived(weights[a][j].at[1 - h, y, c, half], s_wz.at[a, j])
            edge_copy(a, j, True).start()

    def mirror_wait(a, j):
        @pl.when(jnp.logical_not(edge))
        def _():
            arrived(weights[a][j].at[1 - h, y, c, half], s_wz.at[a, j])

    def far_y(a, j, k):
        block = weights[a][j].at[side(k), y, c]
        src = weights_in[a][j]
        if k == 1:
            block = block.at[half]
            src = block
            mirror_wait(a, j)
        for d in (1, 3):
            push(src, block, s_wy.at[a, j, k, d // 2], at(y=y + d))

    def quarter(parity, e):
        return pl.ds(pl.multiple_of(parity * 32 + e * 16, 16), 16)

    def far_push(a, j, k, d):
        for e in range(2):
            block = weights[a][j].at[side(k), (y + d) % 4, c, quarter(p, e)]
            push(block, block, s_wx.at[a, j, k, e, d], at(x=x + (1 if e == 0 else 3)))

    def passed_on(k, e):
        return quarter(p, e) if k == 1 else pl.ds(e * 32, 32)

    def far_f(a, j, k):
        for e in range(2):
            d = 1 if e == 0 else 3
            near = weights[a][j].at[side(k), (y + 4 - d) % 4, c]
            arrived(near.at[half] if k == 1 else near, s_wy.at[a, j, k, e])
            piece = near.at[passed_on(k, e)]
            push(piece, piece, s_wf.at[a, j, k, e], at(y=y + d))
        if k == 1:
            for d in (0, 3, 1):
                far_push(a, j, k, d)

    def far_x(a, j, k):
        for e in range(2):
            arrived(weights[a][j].at[side(k), (y + 2) % 4, c, passed_on(k, e)], s_wf.at[a, j, k, e])
        block = weights[a][j].at[side(k), :, c]
        if k == 0:
            own_copies[a][j].wait()
        else:
            far_push(a, j, k, 2)
            block = weights[a][j].at[side(k), :, c, half]
        push(block, block, s_wd.at[a, j, k, 0], at(c=1 - c))

    def far_d(a, j):
        for d in (0, 3, 1, 2):
            for e in range(2):
                arrived(weights[a][j].at[side(1), (y + d) % 4, c, quarter(1 - p, e)], s_wx.at[a, j, 1, e, d])
        block = weights[a][j].at[side(1), :, c, other_half]
        push(block, block, s_wd.at[a, j, 1, 1], at(c=1 - c))

    def near_y(j, k):
        block = weights[0][j].at[side(k), y, c, half]
        if k == 1:
            mirror_wait(0, j)
        src = weights_in[0][j].at[half] if k == 0 else block
        for d in (1, 3, 2):
            push(src, block, s_ny.at[j, k, d - 1], at(y=y + d))

    def near_x(j, k):
        if k == 0:
            own_copies[0][j].wait()
        for d in (1, 3, 2):
            arrived(weights[0][j].at[side(k), (y + 4 - d) % 4, c, half], s_ny.at[j, k, d - 1])
        for e in range(2):
            block = weights[0][j].at[side(k), :, c, quarter(p, e)]
            push(block, block, s_wx.at[0, j, k, e, 0], at(x=x + (1 if e == 0 else 3)))
        block = weights[0][j].at[side(k), :, c, half]
        push(block, block, s_wd.at[0, j, k, 0], at(c=1 - c))

    def near_d(j, k):
        for e in range(2):
            arrived(weights[0][j].at[side(k), :, c, quarter(1 - p, e)], s_wx.at[0, j, k, e, 0])
        block = weights[0][j].at[side(k), :, c, other_half]
        push(block, block, s_wd.at[0, j, k, 1], at(c=1 - c))

    def weights_ready(a, j):
        for k in range(2):
            if a == 1 and k == 0:
                arrived(weights[a][j].at[side(k), :, 1 - c], s_wd.at[a, j, k, 0])
                continue
            arrived(weights[a][j].at[side(k), :, 1 - c, half], s_wd.at[a, j, k, 0])
            arrived(weights[a][j].at[side(k), :, 1 - c, other_half], s_wd.at[a, j, k, 1])


    def reduce_x(b):
        for d in (1, 3, 2):
            xt = (x + d) % 4
            push(slab.at[xt, :, b], rx.at[d - 1, :, b], s_rx.at[b, d - 1], at(x=xt))

    def reduce_x_arrived(b):
        for d in (1, 3, 2):
            arrived(rx.at[d - 1, :, b], s_rx.at[b, d - 1])

    def reduce_z(b):
        for i in range(4):
            total = slab[x, i, b].astype(F32) + rx[0, i, b].astype(F32)
            total = total + rx[1, i, b].astype(F32) + rx[2, i, b].astype(F32)
            sx[i, b] = total.astype(BF)
        for d in (1, 3, 2):
            zt = (zl + d) % 4
            push(sx.at[zt, b], rz.at[d - 1, b], s_rz.at[b, d - 1], at(z=h * 4 + zt))

    def gather_x(b):
        for d in (1, 3, 2):
            arrived(rz.at[d - 1, b], s_rz.at[b, d - 1])
        total = sx[zl, b].astype(F32) + rz[0, b].astype(F32) + rz[1, b].astype(F32) + rz[2, b].astype(F32)
        total = total * lax.rsqrt(jnp.mean(total * total, axis=-1, keepdims=True) + 1e-06)
        nb[h, x, zl, b] = total.astype(BF)
        piece = nb.at[h, x, zl, b]
        for d in (1, 3, 2):
            push(piece, piece, s_ax.at[b, d - 1], at(x=x + d))

    def gather_x_arrived(b):
        for d in (1, 3, 2):
            arrived(nb.at[h, (x + 4 - d) % 4, zl, b], s_ax.at[b, d - 1])

    def ring_piece(source, t, way, b):
        rows = pl.ds(0, 4) if t < 4 else pl.ds(2 * way, 2)
        return nb.at[source // 4, rows, source % 4, b]

    def ring_send(t, b):
        for way in range(2):
            source = zmod(z - (t - 1)) if way == 0 else zmod(z + (t - 1))
            target = zmod(z + 1) if way == 0 else zmod(z - 1)
            piece = ring_piece(source, t, way, b)
            push(piece, piece, s_az.at[b, t - 1, way], at(z=target))

    def ring_arrived(t, b):
        for way in range(2):
            source = zmod(z - t) if way == 0 else zmod(z + t)
            arrived(ring_piece(source, t, way, b), s_az.at[b, t - 1, way])

    here = pl.ds(pl.multiple_of(h * 2, 2), 2)

    def project(b):
        @pl.loop(0, 8)
        def _(i):
            part = nb[i // 4, i % 4, :, b].reshape(64, C)
            grown = (part.astype(F32) * film_gain + film_bias).astype(BF)
            hid[i // 4, i % 4, :, b] = grown.reshape(4, 16, C)

        @pl.loop(0, 2)
        def _(t):
            block = wqr[:, :, :, :, pl.ds(pl.multiple_of(C + t * TILE, TILE), TILE)].reshape(C, TILE)
            cut = pl.ds(pl.multiple_of(t * TILE, TILE), TILE)
            tokens = hid[:, :, :, b].reshape(512, C)
            grown = jnp.dot(tokens, block, preferred_element_type=F32).astype(BF)
            kv[:, :, :, b, :, cut] = grown.reshape(2, 4, 4, 16, TILE)

        block = wqr[:, :, :, :, :C].reshape(C, C)
        tokens = hid[:, :, here, b].reshape(256, C)
        grown = jnp.dot(tokens, block, preferred_element_type=F32).astype(BF)
        qb[:, :, :, b] = grown.reshape(2, 4, 2, 16, C)

    def row_step(hp):
        for head in range(HEADS):
            cut = slice(head * DIM, (head + 1) * DIM)
            vcut = slice(C + head * DIM, C + (head + 1) * DIM)
            q = qb[hp, :, :, :, :, cut].reshape(4, 64, DIM)
            keys = kv[hp, :, :, :, :, cut].reshape(4, 128, DIM)
            values = kv[hp, :, :, :, :, vcut].reshape(4, 128, DIM)
            mixed[pl.ds(0, 256), cut] = attend(q, keys, values).astype(BF)

        block = wor[...].reshape(C, C)
        grown = jnp.dot(mixed[pl.ds(0, 256), :], block, preferred_element_type=F32)
        grown = (grown + hid[hp, :, here].reshape(256, C).astype(F32)).reshape(4, 64, C)
        for d in range(8):
            send[hp, d] = grown[:, d * 8 : (d + 1) * 8, :].reshape(32, C).astype(BF)

        for dy in (2, 1, 3, 0):
            for dc in range(2):
                if dy == 0 and dc == 0:
                    continue
                ty, tc = (y + dy) % 4, (c + dc) % 2
                push(
                    send.at[hp, ty * 2 + tc], cols.at[hp, yc], s_a2a.at[hp, dy * 2 + dc], at(y=ty, c=tc)
                )
        return pull(send.at[hp, yc], cols.at[hp, yc])

    def row_arrived(hp):
        for dy in (2, 1, 3, 0):
            for dc in range(2):
                if dy == 0 and dc == 0:
                    continue
                sy, sc = (y + 4 - dy) % 4, (c + dc) % 2
                arrived(cols.at[hp, sy * 2 + sc], s_a2a.at[hp, dy * 2 + dc])

    reduce_x(0)
    mirror_send(0, 0)
    near_y(0, 0)
    mirror_send(0, 1)
    mirror_pass(0, 0)
    reduce_x_arrived(0)
    reduce_x(1)
    reduce_z(0)
    mirror_pass(0, 1)
    mirror_send(1, 0)
    mirror_send(1, 1)
    gather_x(0)
    near_y(0, 1)
    near_y(1, 0)
    near_x(0, 0)
    reduce_x_arrived(1)
    reduce_z(1)
    gather_x_arrived(0)
    ring_send(1, 0)
    mirror_pass(1, 0)
    mirror_pass(1, 1)
    gather_x(1)
    near_y(1, 1)
    near_x(0, 1)
    ring_arrived(1, 0)
    ring_send(2, 0)
    gather_x_arrived(1)
    ring_send(1, 1)
    far_y(1, 0, 0)
    near_x(1, 0)
    ring_arrived(2, 0)
    ring_send(3, 0)
    ring_arrived(1, 1)
    ring_send(2, 1)
    near_x(1, 1)
    near_d(0, 0)
    far_y(1, 0, 1)
    ring_arrived(3, 0)
    ring_send(4, 0)
    ring_arrived(2, 1)
    ring_send(3, 1)
    near_d(0, 1)
    far_f(1, 0, 0)
    far_y(1, 1, 0)
    far_y(1, 1, 1)
    ring_arrived(4, 0)
    ring_arrived(3, 1)
    ring_send(4, 1)
    near_d(1, 0)
    near_d(1, 1)
    far_f(1, 0, 1)
    for copy in table_copies:
        copy.wait()
    time = lead_ids[0]
    film_gain = 1.0 + scale_t[pl.ds(time, 1), :]
    film_bias = shift_t[pl.ds(time, 1), :]
    weights_ready(0, 0)
    project(0)
    far_x(1, 0, 0)
    far_x(1, 0, 1)
    far_f(1, 1, 0)
    far_f(1, 1, 1)
    ring_arrived(4, 1)
    project(1)
    far_x(1, 1, 0)
    far_x(1, 1, 1)
    far_d(1, 0)
    weights_ready(0, 1)
    own0 = row_step(0)
    far_d(1, 1)
    own1 = row_step(1)
    def prepare(hp):
        @pl.loop(0, 8)
        def _(i):
            part = cols[hp, i].astype(F32)
            part = part * lax.rsqrt(jnp.mean(part * part, axis=-1, keepdims=True) + 1e-06) * gain[...]
            rows = pl.ds(pl.multiple_of(hp * 256 + i * 32, 32), 32)
            for s in range(8):
                xf[s, rows, :] = part[:, s * DIM : (s + 1) * DIM]

        for w in range(8):
            for s in range(8):
                taken = xf[s, pl.ds(hp * 256 + w, 32, stride=8), :]
                xt[hp, w * 32 : (w + 1) * 32, s * DIM : (s + 1) * DIM] = taken.astype(BF)

        @pl.loop(0, 3)
        def _(t):
            cut = pl.ds(pl.multiple_of(t * TILE, TILE), TILE)
            block = wqc[:, :, :, :, cut].reshape(C, TILE)
            grown = jnp.dot(xt[hp], block, preferred_element_type=F32).astype(BF)
            kvc[:, hp, :, cut] = grown.reshape(8, 32, TILE)

    own0.wait()
    row_arrived(0)
    weights_ready(1, 0)
    prepare(0)
    own1.wait()
    row_arrived(1)
    prepare(1)

    for head in range(HEADS):
        cut = slice(head * DIM, (head + 1) * DIM)
        q, keys, values = (
            kvc[:, :, :, i * C + head * DIM : i * C + (head + 1) * DIM].reshape(8, 64, DIM) for i in range(3)
        )
        mix = attend(q, keys, values)
        for w in range(8):
            xf[head, pl.ds(w, 64, stride=8), :] = mix[w * 64 : (w + 1) * 64]
        mixed[:, cut] = xf[head].astype(BF)

    weights_ready(1, 1)
    block = woc[...].reshape(C, C)
    grown = jnp.dot(mixed[...], block, preferred_element_type=F32)
    out[...] = (grown + cols[...].reshape(512, C).astype(F32)).astype(BF)

    for copy in started:
        copy.wait_send()

    @pl.when(edge)
    def _():
        for a in range(2):
            for j in range(2):
                for forward in (False, True):
                    edge_copy(a, j, forward).wait_send()


def on_device(
    latents, owners, lead_ids, film_scale, film_shift, w_qkv_row, w_out_row, gain_col, w_qkv_col, w_out_col
):
    anywhere = pl.BlockSpec(memory_space=pl.ANY)
    scalars = pl.BlockSpec(memory_space=pltpu.SMEM)
    vector = pl.BlockSpec(memory_space=pltpu.VMEM)
    dma = pltpu.SemaphoreType.DMA
    result = pl.pallas_call(
        kernel,
        out_shape=jax.ShapeDtypeStruct((512, C), BF),
        in_specs=[
            anywhere, scalars, scalars, anywhere, anywhere, anywhere, anywhere, vector, anywhere, anywhere
        ],
        out_specs=vector,
        scratch_shapes=[
            pltpu.VMEM((4, 4, 2, 16, C), BF),
            pltpu.VMEM((360, C), F32),
            pltpu.VMEM((360, C), F32),
            pltpu.VMEM((3, 4, 2, 16, C), BF),
            pltpu.VMEM((4, 2, 16, C), BF),
            pltpu.VMEM((3, 2, 16, C), BF),
            pltpu.VMEM((2, 4, 4, 2, 16, C), BF),
            pltpu.VMEM((2, 4, 4, 2, 16, C), BF),
            pltpu.VMEM((2, 256, C), BF),
            pltpu.VMEM((2, 4, 4, 2, 16, 2 * C), BF),
            pltpu.VMEM((8, 2, 32, 3 * C), BF),
            pltpu.VMEM((2, 4, 2, 2, 16, C), BF),
            pltpu.VMEM((512, C), BF),
            pltpu.VMEM((2, 8, 32, C), BF),
            pltpu.VMEM((2, 8, 32, C), BF),
            pltpu.VMEM((8, 512, DIM), F32),
            pltpu.VMEM((2, 4, 2, 64, 3 * C), BF),
            pltpu.VMEM((2, 4, 2, 64, C), BF),
            pltpu.VMEM((2, 4, 2, 64, 3 * C), BF),
            pltpu.VMEM((2, 4, 2, 64, C), BF),
            dma((SENDS,)),
            dma((9,)),
            dma((2, 3)),
            dma((2, 3)),
            dma((2, 3)),
            dma((2, 4, 2)),
            dma((2, 2, 2)),
            dma((2, 2, 3)),
            dma((2, 2)),
            dma((2, 2, 2, 2)),
            dma((2, 2, 2, 2)),
            dma((2, 2, 2, 2, 4)),
            dma((2, 2, 2, 2)),
            dma((2, 8)),
        ],
        compiler_params=pltpu.CompilerParams(
            collective_id=0, has_side_effects=True, vmem_limit_bytes=56 << 20
        ),
        name="axial_attention",
    )(
        latents.reshape(4, 4, 2, 16, C), owners, lead_ids, film_scale, film_shift,
        w_qkv_row, w_out_row, gain_col.reshape(1, C), w_qkv_col, w_out_col,
    )
    return result.reshape(1, 64, 8, C)


def solution(mesh):
    placed = (
        P("lead", "space", None, None),
        P(),
        P("lead"),
        P(),
        P(),
        P("space", None),
        P("space", None),
        P(),
        P("space", None),
        P("space", None),
    )
    return jax.shard_map(
        on_device,
        mesh=mesh,
        in_specs=placed,
        out_specs=P("lead", None, "space", None),
        check_vma=False,
    )
```

```python
import functools

import jax
import jax.numpy as jnp
from jax import lax
from jax.experimental import pallas as pl
from jax.experimental.pallas import tpu as pltpu
from jax.sharding import PartitionSpec as P

HEADS = 8
DIM = 128
C = 1024
MESH = pl.DeviceIdType.MESH
BF = jnp.bfloat16
F32 = jnp.float32
SENDS = 200


def attend(q, keys, values):
    batch, count, _ = q.shape
    scores = lax.dot_general(q, keys, (((2,), (2,)), ((0,), (0,))), preferred_element_type=F32)
    top = jnp.max(scores, axis=-1, keepdims=True)
    weights = jnp.exp((scores - top) * (DIM**-0.5)).astype(BF)
    mix = lax.dot_general(weights, values, (((2,), (1,)), ((0,), (0,))), preferred_element_type=F32)
    ones = jnp.ones((keys.shape[1], DIM), BF)
    total = jnp.dot(weights.reshape(batch * count, keys.shape[1]), ones, preferred_element_type=F32)
    return mix.reshape(batch * count, DIM) / total


def kernel(
    slab_in, owners, lead_ids, scale_in, shift_in, wqr_in, wor_in, gain, wqc_in, woc_in,
    out,
    slab, scale_t, shift_t, rx, sx, rz, nb, hid, xt, kv, kvc, qb, mixed, send, cols, xf,
    wqr, wor, wqc, woc,
    ssem, loc, s_rx, s_rz, s_ax, s_az, s_edge, s_ny, s_wz, s_wy, s_wf, s_wx, s_wd, s_a2a,
):
    lead = lax.axis_index("lead")
    space = lax.axis_index("space")
    x, zl = lead // 4, lead % 4
    h, y, c = space // 8, (space // 2) % 4, space % 2
    z = h * 4 + zl
    p = x % 2
    yc = space % 8

    def at(x=x, y=y, z=z, c=c):
        return ((x % 4) * 4 + z % 4, (z // 4) * 8 + (y % 4) * 2 + c)

    def zmod(v):
        return (v + 8) % 8

    started = []

    def push(src, dst, recv, dev):
        copy = pltpu.make_async_remote_copy(
            src, dst, ssem.at[len(started)], recv, device_id=dev, device_id_type=MESH
        )
        copy.start()
        started.append(copy)

    def arrived(dst, recv):
        pltpu.make_async_remote_copy(
            dst, dst, ssem.at[0], recv, device_id=at(c=1 - c), device_id_type=MESH
        ).wait_recv()

    weights_in = ((wqr_in, wor_in), (wqc_in, woc_in))
    weights = ((wqr, wor), (wqc, woc))

    local = []

    def pull(src, dst):
        copy = pltpu.make_async_copy(src, dst, loc.at[len(local)])
        copy.start()
        local.append(copy)
        return copy

    slab_copy = pull(slab_in.at[x], slab)
    half = pl.ds(pl.multiple_of(p * 32, 32), 32)
    other_half = pl.ds(pl.multiple_of((1 - p) * 32, 32), 32)
    own_copies = [
        [pull(weights_in[0][j].at[half], weights[0][j].at[h, y, c, half]) for j in range(2)],
        [pull(weights_in[1][j], weights[1][j].at[h, y, c]) for j in range(2)],
    ]
    table_copies = [pull(scale_in, scale_t), pull(shift_in, shift_t)]

    barrier = pltpu.get_barrier_semaphore()
    peers = [at(x=x + d) for d in range(1, 4)]
    peers += [at(y=y + d) for d in range(1, 4)]
    peers += [at(z=h * 4 + (zl + d) % 4) for d in range(1, 4)]
    peers += [at(z=7 - z), at(c=1 - c)]
    for peer in peers:
        pl.semaphore_signal(barrier, 1, device_id=peer, device_id_type=MESH)
    pl.semaphore_wait(barrier, len(peers))

    def side(k):
        return h if k == 0 else 1 - h

    edge = jnp.logical_or(zl == 0, zl == 3)
    inner = h * 4 + jnp.where(zl == 0, 1, 2)

    def edge_copy(a, j, forward):
        own = weights_in[a][j].at[half]
        there = weights[a][j].at[h, y, c, half]
        far = weights[a][j].at[1 - h, y, c, half]
        return pltpu.make_async_remote_copy(
            far if forward else own,
            far if forward else there,
            s_edge.at[a, j, int(forward)],
            s_wz.at[a, j],
            device_id=at(z=inner if forward else 7 - z),
            device_id_type=MESH,
        )

    def mirror_send(a, j):
        @pl.when(edge)
        def _():
            edge_copy(a, j, False).start()

    def mirror_pass(a, j):
        @pl.when(edge)
        def _():
            arrived(weights[a][j].at[1 - h, y, c, half], s_wz.at[a, j])
            edge_copy(a, j, True).start()

    def mirror_wait(a, j):
        @pl.when(jnp.logical_not(edge))
        def _():
            arrived(weights[a][j].at[1 - h, y, c, half], s_wz.at[a, j])

    def far_y(a, j, k):
        block = weights[a][j].at[side(k), y, c]
        src = weights_in[a][j]
        if k == 1:
            block = block.at[half]
            src = block
            mirror_wait(a, j)
        for d in (1, 3):
            push(src, block, s_wy.at[a, j, k, d // 2], at(y=y + d))

    def quarter(parity, e):
        return pl.ds(pl.multiple_of(parity * 32 + e * 16, 16), 16)

    def far_push(a, j, k, d):
        for e in range(2):
            block = weights[a][j].at[side(k), (y + d) % 4, c, quarter(p, e)]
            push(block, block, s_wx.at[a, j, k, e, d], at(x=x + (1 if e == 0 else 3)))

    def passed_on(k, e):
        return quarter(p, e) if k == 1 else pl.ds(e * 32, 32)

    def far_f(a, j, k):
        for e in range(2):
            d = 1 if e == 0 else 3
            near = weights[a][j].at[side(k), (y + 4 - d) % 4, c]
            arrived(near.at[half] if k == 1 else near, s_wy.at[a, j, k, e])
            piece = near.at[passed_on(k, e)]
            push(piece, piece, s_wf.at[a, j, k, e], at(y=y + d))
        if k == 1:
            for d in (0, 3, 1):
                far_push(a, j, k, d)

    def far_x(a, j, k):
        for e in range(2):
            arrived(weights[a][j].at[side(k), (y + 2) % 4, c, passed_on(k, e)], s_wf.at[a, j, k, e])
        block = weights[a][j].at[side(k), :, c]
        if k == 0:
            own_copies[a][j].wait()
        else:
            far_push(a, j, k, 2)
            block = weights[a][j].at[side(k), :, c, half]
        push(block, block, s_wd.at[a, j, k, 0], at(c=1 - c))

    def far_d(a, j):
        for d in (0, 3, 1, 2):
            for e in range(2):
                arrived(weights[a][j].at[side(1), (y + d) % 4, c, quarter(1 - p, e)], s_wx.at[a, j, 1, e, d])
        block = weights[a][j].at[side(1), :, c, other_half]
        push(block, block, s_wd.at[a, j, 1, 1], at(c=1 - c))

    def near_y(j, k):
        block = weights[0][j].at[side(k), y, c, half]
        if k == 1:
            mirror_wait(0, j)
        src = weights_in[0][j].at[half] if k == 0 else block
        for d in (1, 3, 2):
            push(src, block, s_ny.at[j, k, d - 1], at(y=y + d))

    def near_x(j, k):
        if k == 0:
            own_copies[0][j].wait()
        for d in (1, 3, 2):
            arrived(weights[0][j].at[side(k), (y + 4 - d) % 4, c, half], s_ny.at[j, k, d - 1])
        for e in range(2):
            block = weights[0][j].at[side(k), :, c, quarter(p, e)]
            push(block, block, s_wx.at[0, j, k, e, 0], at(x=x + (1 if e == 0 else 3)))
        block = weights[0][j].at[side(k), :, c, half]
        push(block, block, s_wd.at[0, j, k, 0], at(c=1 - c))

    def near_d(j, k):
        for e in range(2):
            arrived(weights[0][j].at[side(k), :, c, quarter(1 - p, e)], s_wx.at[0, j, k, e, 0])
        block = weights[0][j].at[side(k), :, c, other_half]
        push(block, block, s_wd.at[0, j, k, 1], at(c=1 - c))

    def weights_ready(a, j):
        for k in range(2):
            if a == 1 and k == 0:
                arrived(weights[a][j].at[side(k), :, 1 - c], s_wd.at[a, j, k, 0])
                continue
            arrived(weights[a][j].at[side(k), :, 1 - c, half], s_wd.at[a, j, k, 0])
            arrived(weights[a][j].at[side(k), :, 1 - c, other_half], s_wd.at[a, j, k, 1])


    def reduce_x(b):
        for d in (1, 3, 2):
            xt = (x + d) % 4
            push(slab_in.at[xt, :, b], rx.at[d - 1, :, b], s_rx.at[b, d - 1], at(x=xt))

    def reduce_x_arrived(b):
        for d in (1, 3, 2):
            arrived(rx.at[d - 1, :, b], s_rx.at[b, d - 1])

    def kept(d):
        source = (x + 4 - d) % 4 * 4 + zl
        return jnp.where(jnp.logical_or(owners[0] == source, owners[1] == source), 1.0, 0.0).astype(F32)

    def reduce_z(b):
        for i in range(4):
            total = slab[i, b].astype(F32) * kept(0)
            for d in range(1, 4):
                total = total + rx[d - 1, i, b].astype(F32) * kept(d)
            sx[i, b] = total.astype(BF)
        for d in (1, 3, 2):
            zt = (zl + d) % 4
            push(sx.at[zt, b], rz.at[d - 1, b], s_rz.at[b, d - 1], at(z=h * 4 + zt))

    def gather_x(b):
        for d in (1, 3, 2):
            arrived(rz.at[d - 1, b], s_rz.at[b, d - 1])
        total = sx[zl, b].astype(F32) + rz[0, b].astype(F32) + rz[1, b].astype(F32) + rz[2, b].astype(F32)
        total = total * lax.rsqrt(jnp.mean(total * total, axis=-1, keepdims=True) + 1e-06)
        nb[h, x, zl, b] = total.astype(BF)
        piece = nb.at[h, x, zl, b]
        for d in (1, 3, 2):
            push(piece, piece, s_ax.at[b, d - 1], at(x=x + d))

    def gather_x_arrived(b):
        for d in (1, 3, 2):
            arrived(nb.at[h, (x + 4 - d) % 4, zl, b], s_ax.at[b, d - 1])

    def ring_piece(source, t, way, b):
        rows = pl.ds(0, 4) if t < 4 else pl.ds(2 * way, 2)
        return nb.at[source // 4, rows, source % 4, b]

    def ring_send(t, b):
        for way in range(2):
            source = zmod(z - (t - 1)) if way == 0 else zmod(z + (t - 1))
            target = zmod(z + 1) if way == 0 else zmod(z - 1)
            piece = ring_piece(source, t, way, b)
            push(piece, piece, s_az.at[b, t - 1, way], at(z=target))

    def ring_arrived(t, b):
        for way in range(2):
            source = zmod(z - t) if way == 0 else zmod(z + t)
            arrived(ring_piece(source, t, way, b), s_az.at[b, t - 1, way])

    here = pl.ds(pl.multiple_of(h * 2, 2), 2)

    def project(b):
        @pl.loop(0, 8)
        def _(i):
            part = nb[i // 4, i % 4, :, b].reshape(64, C)
            grown = (part.astype(F32) * film_gain + film_bias).astype(BF)
            hid[i // 4, i % 4, :, b] = grown.reshape(4, 16, C)

        block = wqr[:, :, :, :, C:].reshape(C, 2 * C)
        grown = jnp.dot(hid[:, :, :, b].reshape(512, C), block, preferred_element_type=F32).astype(BF)
        kv[:, :, :, b] = grown.reshape(2, 4, 4, 16, 2 * C)

        block = wqr[:, :, :, :, :C].reshape(C, C)
        tokens = hid[:, :, here, b].reshape(256, C)
        grown = jnp.dot(tokens, block, preferred_element_type=F32).astype(BF)
        qb[:, :, :, b] = grown.reshape(2, 4, 2, 16, C)

    def row_step(hp):
        for head in range(HEADS):
            cut = slice(head * DIM, (head + 1) * DIM)
            vcut = slice(C + head * DIM, C + (head + 1) * DIM)
            q = qb[hp, :, :, :, :, cut].reshape(4, 64, DIM)
            keys = kv[hp, :, :, :, :, cut].reshape(4, 128, DIM)
            values = kv[hp, :, :, :, :, vcut].reshape(4, 128, DIM)
            mixed[pl.ds(0, 256), cut] = attend(q, keys, values).astype(BF)

        block = wor[...].reshape(C, C)
        grown = jnp.dot(mixed[pl.ds(0, 256), :], block, preferred_element_type=F32)
        grown = (grown + hid[hp, :, here].reshape(256, C).astype(F32)).reshape(4, 64, C)
        for d in range(8):
            send[hp, d] = grown[:, d * 8 : (d + 1) * 8, :].reshape(32, C).astype(BF)

        for dy in (2, 1, 3, 0):
            for dc in range(2):
                if dy == 0 and dc == 0:
                    continue
                ty, tc = (y + dy) % 4, (c + dc) % 2
                push(
                    send.at[hp, ty * 2 + tc], cols.at[hp, yc], s_a2a.at[hp, dy * 2 + dc], at(y=ty, c=tc)
                )
        return pull(send.at[hp, yc], cols.at[hp, yc])

    def row_arrived(hp):
        for dy in (2, 1, 3, 0):
            for dc in range(2):
                if dy == 0 and dc == 0:
                    continue
                sy, sc = (y + 4 - dy) % 4, (c + dc) % 2
                arrived(cols.at[hp, sy * 2 + sc], s_a2a.at[hp, dy * 2 + dc])

    reduce_x(0)
    mirror_send(0, 0)
    near_y(0, 0)
    mirror_send(0, 1)
    mirror_pass(0, 0)
    reduce_x_arrived(0)
    reduce_x(1)
    slab_copy.wait()
    reduce_z(0)
    mirror_pass(0, 1)
    mirror_send(1, 0)
    mirror_send(1, 1)
    gather_x(0)
    near_y(0, 1)
    near_y(1, 0)
    near_x(0, 0)
    reduce_x_arrived(1)
    reduce_z(1)
    gather_x_arrived(0)
    ring_send(1, 0)
    mirror_pass(1, 0)
    mirror_pass(1, 1)
    gather_x(1)
    near_y(1, 1)
    near_x(0, 1)
    ring_arrived(1, 0)
    ring_send(2, 0)
    gather_x_arrived(1)
    ring_send(1, 1)
    far_y(1, 0, 0)
    near_x(1, 0)
    ring_arrived(2, 0)
    ring_send(3, 0)
    ring_arrived(1, 1)
    ring_send(2, 1)
    near_x(1, 1)
    near_d(0, 0)
    far_y(1, 0, 1)
    ring_arrived(3, 0)
    ring_send(4, 0)
    ring_arrived(2, 1)
    ring_send(3, 1)
    near_d(0, 1)
    far_f(1, 0, 0)
    far_y(1, 1, 0)
    far_y(1, 1, 1)
    ring_arrived(4, 0)
    ring_arrived(3, 1)
    ring_send(4, 1)
    near_d(1, 0)
    near_d(1, 1)
    far_f(1, 0, 1)
    for copy in table_copies:
        copy.wait()
    time = lead_ids[0]
    film_gain = 1.0 + scale_t[pl.ds(time, 1), :]
    film_bias = shift_t[pl.ds(time, 1), :]
    weights_ready(0, 0)
    project(0)
    far_x(1, 0, 0)
    far_x(1, 0, 1)
    far_f(1, 1, 0)
    far_f(1, 1, 1)
    ring_arrived(4, 1)
    project(1)
    far_x(1, 1, 0)
    far_x(1, 1, 1)
    far_d(1, 0)
    weights_ready(0, 1)
    own0 = row_step(0)
    far_d(1, 1)
    own1 = row_step(1)
    def prepare(hp):
        @pl.loop(0, 8)
        def _(i):
            part = cols[hp, i].astype(F32)
            part = part * lax.rsqrt(jnp.mean(part * part, axis=-1, keepdims=True) + 1e-06) * gain[...]
            rows = pl.ds(pl.multiple_of(hp * 256 + i * 32, 32), 32)
            for s in range(8):
                xf[s, rows, :] = part[:, s * DIM : (s + 1) * DIM]

        for w in range(8):
            for s in range(8):
                taken = xf[s, pl.ds(hp * 256 + w, 32, stride=8), :]
                xt[hp, w * 32 : (w + 1) * 32, s * DIM : (s + 1) * DIM] = taken.astype(BF)

        grown = jnp.dot(xt[hp], wqc[...].reshape(C, 3 * C), preferred_element_type=F32).astype(BF)
        kvc[:, hp] = grown.reshape(8, 32, 3 * C)

    own0.wait()
    row_arrived(0)
    weights_ready(1, 0)
    prepare(0)
    own1.wait()
    row_arrived(1)
    prepare(1)

    for head in range(HEADS):
        cut = slice(head * DIM, (head + 1) * DIM)
        q, keys, values = (
            kvc[:, :, :, i * C + head * DIM : i * C + (head + 1) * DIM].reshape(8, 64, DIM) for i in range(3)
        )
        mix = attend(q, keys, values)
        for w in range(8):
            xf[head, pl.ds(w, 64, stride=8), :] = mix[w * 64 : (w + 1) * 64]
        mixed[:, cut] = xf[head].astype(BF)

    weights_ready(1, 1)
    block = woc[...].reshape(C, C)
    grown = jnp.dot(mixed[...], block, preferred_element_type=F32)
    out[...] = (grown + cols[...].reshape(512, C).astype(F32)).astype(BF)

    for copy in started:
        copy.wait_send()

    @pl.when(edge)
    def _():
        for a in range(2):
            for j in range(2):
                for forward in (False, True):
                    edge_copy(a, j, forward).wait_send()


def on_device(
    latents, owners, lead_ids, film_scale, film_shift, w_qkv_row, w_out_row, gain_col, w_qkv_col, w_out_col
):
    anywhere = pl.BlockSpec(memory_space=pl.ANY)
    scalars = pl.BlockSpec(memory_space=pltpu.SMEM)
    vector = pl.BlockSpec(memory_space=pltpu.VMEM)
    dma = pltpu.SemaphoreType.DMA
    result = pl.pallas_call(
        kernel,
        out_shape=jax.ShapeDtypeStruct((512, C), BF),
        in_specs=[
            anywhere, scalars, scalars, anywhere, anywhere, anywhere, anywhere, vector, anywhere, anywhere
        ],
        out_specs=vector,
        scratch_shapes=[
            pltpu.VMEM((4, 2, 16, C), BF),
            pltpu.VMEM((360, C), F32),
            pltpu.VMEM((360, C), F32),
            pltpu.VMEM((3, 4, 2, 16, C), BF),
            pltpu.VMEM((4, 2, 16, C), BF),
            pltpu.VMEM((3, 2, 16, C), BF),
            pltpu.VMEM((2, 4, 4, 2, 16, C), BF),
            pltpu.VMEM((2, 4, 4, 2, 16, C), BF),
            pltpu.VMEM((2, 256, C), BF),
            pltpu.VMEM((2, 4, 4, 2, 16, 2 * C), BF),
            pltpu.VMEM((8, 2, 32, 3 * C), BF),
            pltpu.VMEM((2, 4, 2, 2, 16, C), BF),
            pltpu.VMEM((512, C), BF),
            pltpu.VMEM((2, 8, 32, C), BF),
            pltpu.VMEM((2, 8, 32, C), BF),
            pltpu.VMEM((8, 512, DIM), F32),
            pltpu.VMEM((2, 4, 2, 64, 3 * C), BF),
            pltpu.VMEM((2, 4, 2, 64, C), BF),
            pltpu.VMEM((2, 4, 2, 64, 3 * C), BF),
            pltpu.VMEM((2, 4, 2, 64, C), BF),
            dma((SENDS,)),
            dma((9,)),
            dma((2, 3)),
            dma((2, 3)),
            dma((2, 3)),
            dma((2, 4, 2)),
            dma((2, 2, 2)),
            dma((2, 2, 3)),
            dma((2, 2)),
            dma((2, 2, 2, 2)),
            dma((2, 2, 2, 2)),
            dma((2, 2, 2, 2, 4)),
            dma((2, 2, 2, 2)),
            dma((2, 8)),
        ],
        compiler_params=pltpu.CompilerParams(
            collective_id=0, has_side_effects=True, vmem_limit_bytes=56 << 20
        ),
        name="axial_attention",
    )(
        latents.reshape(4, 4, 2, 16, C), owners, lead_ids, film_scale, film_shift,
        w_qkv_row, w_out_row, gain_col.reshape(1, C), w_qkv_col, w_out_col,
    )
    return result.reshape(1, 64, 8, C)


def solution(mesh):
    placed = (
        P("lead", "space", None, None),
        P(),
        P("lead"),
        P(),
        P(),
        P("space", None),
        P("space", None),
        P(),
        P("space", None),
        P("space", None),
    )
    return jax.shard_map(
        on_device,
        mesh=mesh,
        in_specs=placed,
        out_specs=P("lead", None, "space", None),
        check_vma=False,
    )
```

```python
import functools

import jax
import jax.numpy as jnp
from jax import lax
from jax.experimental import pallas as pl
from jax.experimental.pallas import tpu as pltpu
from jax.sharding import PartitionSpec as P

HEADS = 8
DIM = 128
C = 1024
MESH = pl.DeviceIdType.MESH
BF = jnp.bfloat16
F32 = jnp.float32
SENDS = 200


def attend(q, keys, values):
    batch, count, _ = q.shape
    scores = lax.dot_general(q, keys, (((2,), (2,)), ((0,), (0,))), preferred_element_type=F32)
    top = jnp.max(scores, axis=-1, keepdims=True)
    weights = jnp.exp((scores - top) * (DIM**-0.5)).astype(BF)
    mix = lax.dot_general(weights, values, (((2,), (1,)), ((0,), (0,))), preferred_element_type=F32)
    ones = jnp.ones((keys.shape[1], DIM), BF)
    total = jnp.dot(weights.reshape(batch * count, keys.shape[1]), ones, preferred_element_type=F32)
    return mix.reshape(batch * count, DIM) / total


def kernel(
    slab_in, owners, lead_ids, scale_in, shift_in, wqr_in, wor_in, gain, wqc_in, woc_in,
    out,
    stage, slab, scale_t, shift_t, rx, sx, rz, nb, hid, xt, kv, kvc, qb, mixed, send, cols, xf,
    wqr, wor, wqc, woc,
    ssem, loc, s_rx, s_rz, s_ax, s_az, s_edge, s_ny, s_wz, s_wy, s_wf, s_wx, s_wd, s_a2a,
):
    lead = lax.axis_index("lead")
    space = lax.axis_index("space")
    x, zl = lead // 4, lead % 4
    h, y, c = space // 8, (space // 2) % 4, space % 2
    z = h * 4 + zl
    p = x % 2
    yc = space % 8

    def at(x=x, y=y, z=z, c=c):
        return ((x % 4) * 4 + z % 4, (z // 4) * 8 + (y % 4) * 2 + c)

    def zmod(v):
        return (v + 8) % 8

    started = []

    def push(src, dst, recv, dev):
        copy = pltpu.make_async_remote_copy(
            src, dst, ssem.at[len(started)], recv, device_id=dev, device_id_type=MESH
        )
        copy.start()
        started.append(copy)

    def arrived(dst, recv):
        pltpu.make_async_remote_copy(
            dst, dst, ssem.at[0], recv, device_id=at(c=1 - c), device_id_type=MESH
        ).wait_recv()

    weights_in = ((wqr_in, wor_in), (wqc_in, woc_in))
    weights = ((wqr, wor), (wqc, woc))

    local = []

    def pull(src, dst):
        copy = pltpu.make_async_copy(src, dst, loc.at[len(local)])
        copy.start()
        local.append(copy)
        return copy

    slab_copy = pull(slab_in.at[x], slab)
    half = pl.ds(pl.multiple_of(p * 32, 32), 32)
    other_half = pl.ds(pl.multiple_of((1 - p) * 32, 32), 32)
    own_copies = [
        [pull(weights_in[0][j].at[half], weights[0][j].at[h, y, c, half]) for j in range(2)],
        [pull(weights_in[1][j], weights[1][j].at[h, y, c]) for j in range(2)],
    ]
    table_copies = [pull(scale_in, scale_t), pull(shift_in, shift_t)]

    barrier = pltpu.get_barrier_semaphore()
    peers = [at(x=x + d) for d in range(1, 4)]
    peers += [at(y=y + d) for d in range(1, 4)]
    peers += [at(z=h * 4 + (zl + d) % 4) for d in range(1, 4)]
    peers += [at(z=7 - z), at(c=1 - c)]
    for peer in peers:
        pl.semaphore_signal(barrier, 1, device_id=peer, device_id_type=MESH)
    pl.semaphore_wait(barrier, len(peers))

    def side(k):
        return h if k == 0 else 1 - h

    edge = jnp.logical_or(zl == 0, zl == 3)
    inner = h * 4 + jnp.where(zl == 0, 1, 2)

    def edge_copy(a, j, forward):
        own = weights_in[a][j].at[half]
        there = weights[a][j].at[h, y, c, half]
        far = weights[a][j].at[1 - h, y, c, half]
        return pltpu.make_async_remote_copy(
            far if forward else own,
            far if forward else there,
            s_edge.at[a, j, int(forward)],
            s_wz.at[a, j],
            device_id=at(z=inner if forward else 7 - z),
            device_id_type=MESH,
        )

    def mirror_send(a, j):
        @pl.when(edge)
        def _():
            edge_copy(a, j, False).start()

    def mirror_pass(a, j):
        @pl.when(edge)
        def _():
            arrived(weights[a][j].at[1 - h, y, c, half], s_wz.at[a, j])
            edge_copy(a, j, True).start()

    def mirror_wait(a, j):
        @pl.when(jnp.logical_not(edge))
        def _():
            arrived(weights[a][j].at[1 - h, y, c, half], s_wz.at[a, j])

    def far_y(a, j, k):
        block = weights[a][j].at[side(k), y, c]
        src = weights_in[a][j]
        if k == 1:
            block = block.at[half]
            src = block
            mirror_wait(a, j)
        for d in (1, 3):
            push(src, block, s_wy.at[a, j, k, d // 2], at(y=y + d))

    def quarter(parity, e):
        return pl.ds(pl.multiple_of(parity * 32 + e * 16, 16), 16)

    def far_push(a, j, k, d):
        for e in range(2):
            block = weights[a][j].at[side(k), (y + d) % 4, c, quarter(p, e)]
            push(block, block, s_wx.at[a, j, k, e, d], at(x=x + (1 if e == 0 else 3)))

    def passed_on(k, e):
        return quarter(p, e) if k == 1 else pl.ds(e * 32, 32)

    def far_f(a, j, k):
        for e in range(2):
            d = 1 if e == 0 else 3
            near = weights[a][j].at[side(k), (y + 4 - d) % 4, c]
            arrived(near.at[half] if k == 1 else near, s_wy.at[a, j, k, e])
            piece = near.at[passed_on(k, e)]
            push(piece, piece, s_wf.at[a, j, k, e], at(y=y + d))
        if k == 1:
            for d in (0, 3, 1):
                far_push(a, j, k, d)

    def far_x(a, j, k):
        for e in range(2):
            arrived(weights[a][j].at[side(k), (y + 2) % 4, c, passed_on(k, e)], s_wf.at[a, j, k, e])
        block = weights[a][j].at[side(k), :, c]
        if k == 0:
            own_copies[a][j].wait()
        else:
            far_push(a, j, k, 2)
            block = weights[a][j].at[side(k), :, c, half]
        push(block, block, s_wd.at[a, j, k, 0], at(c=1 - c))

    def far_d(a, j):
        for d in (0, 3, 1, 2):
            for e in range(2):
                arrived(weights[a][j].at[side(1), (y + d) % 4, c, quarter(1 - p, e)], s_wx.at[a, j, 1, e, d])
        block = weights[a][j].at[side(1), :, c, other_half]
        push(block, block, s_wd.at[a, j, 1, 1], at(c=1 - c))

    def near_y(j, k):
        block = weights[0][j].at[side(k), y, c, half]
        if k == 1:
            mirror_wait(0, j)
        src = weights_in[0][j].at[half] if k == 0 else block
        for d in (1, 3, 2):
            push(src, block, s_ny.at[j, k, d - 1], at(y=y + d))

    def near_x(j, k):
        if k == 0:
            own_copies[0][j].wait()
        for d in (1, 3, 2):
            arrived(weights[0][j].at[side(k), (y + 4 - d) % 4, c, half], s_ny.at[j, k, d - 1])
        for e in range(2):
            block = weights[0][j].at[side(k), :, c, quarter(p, e)]
            push(block, block, s_wx.at[0, j, k, e, 0], at(x=x + (1 if e == 0 else 3)))
        block = weights[0][j].at[side(k), :, c, half]
        push(block, block, s_wd.at[0, j, k, 0], at(c=1 - c))

    def near_d(j, k):
        for e in range(2):
            arrived(weights[0][j].at[side(k), :, c, quarter(1 - p, e)], s_wx.at[0, j, k, e, 0])
        block = weights[0][j].at[side(k), :, c, other_half]
        push(block, block, s_wd.at[0, j, k, 1], at(c=1 - c))

    def weights_ready(a, j):
        for k in range(2):
            if a == 1 and k == 0:
                arrived(weights[a][j].at[side(k), :, 1 - c], s_wd.at[a, j, k, 0])
                continue
            arrived(weights[a][j].at[side(k), :, 1 - c, half], s_wd.at[a, j, k, 0])
            arrived(weights[a][j].at[side(k), :, 1 - c, other_half], s_wd.at[a, j, k, 1])


    def reduce_x(b):
        for d in (1, 3, 2):
            xt = (x + d) % 4
            push(slab_in.at[xt, :, b], rx.at[d - 1, :, b], s_rx.at[b, d - 1], at(x=xt))

    def reduce_x_arrived(b):
        for d in (1, 3, 2):
            arrived(rx.at[d - 1, :, b], s_rx.at[b, d - 1])

    def kept(d):
        source = (x + 4 - d) % 4 * 4 + zl
        return jnp.where(jnp.logical_or(owners[0] == source, owners[1] == source), 1.0, 0.0).astype(F32)

    def reduce_z(b):
        for i in range(4):
            total = slab[i, b].astype(F32) * kept(0)
            for d in range(1, 4):
                total = total + rx[d - 1, i, b].astype(F32) * kept(d)
            sx[i, b] = total.astype(BF)
        for d in (1, 3, 2):
            zt = (zl + d) % 4
            push(sx.at[zt, b], rz.at[d - 1, b], s_rz.at[b, d - 1], at(z=h * 4 + zt))

    def gather_x(b):
        for d in (1, 3, 2):
            arrived(rz.at[d - 1, b], s_rz.at[b, d - 1])
        total = sx[zl, b].astype(F32) + rz[0, b].astype(F32) + rz[1, b].astype(F32) + rz[2, b].astype(F32)
        total = total * lax.rsqrt(jnp.mean(total * total, axis=-1, keepdims=True) + 1e-06)
        nb[h, x, zl, b] = total.astype(BF)
        piece = nb.at[h, x, zl, b]
        for d in (1, 3, 2):
            push(piece, piece, s_ax.at[b, d - 1], at(x=x + d))

    def gather_x_arrived(b):
        for d in (1, 3, 2):
            arrived(nb.at[h, (x + 4 - d) % 4, zl, b], s_ax.at[b, d - 1])

    def ring_piece(source, t, way, b):
        rows = pl.ds(0, 4) if t < 4 else pl.ds(2 * way, 2)
        return nb.at[source // 4, rows, source % 4, b]

    def ring_send(t, b):
        for way in range(2):
            source = zmod(z - (t - 1)) if way == 0 else zmod(z + (t - 1))
            target = zmod(z + 1) if way == 0 else zmod(z - 1)
            piece = ring_piece(source, t, way, b)
            push(piece, piece, s_az.at[b, t - 1, way], at(z=target))

    def ring_arrived(t, b):
        for way in range(2):
            source = zmod(z - t) if way == 0 else zmod(z + t)
            arrived(ring_piece(source, t, way, b), s_az.at[b, t - 1, way])

    here = pl.ds(pl.multiple_of(h * 2, 2), 2)

    def project(b):
        @pl.loop(0, 8)
        def _(i):
            part = nb[i // 4, i % 4, :, b].reshape(64, C)
            grown = (part.astype(F32) * film_gain + film_bias).astype(BF)
            hid[i // 4, i % 4, :, b] = grown.reshape(4, 16, C)

        block = wqr[:, :, :, :, C:].reshape(C, 2 * C)
        grown = jnp.dot(hid[:, :, :, b].reshape(512, C), block, preferred_element_type=F32).astype(BF)
        kv[:, :, :, b] = grown.reshape(2, 4, 4, 16, 2 * C)

        block = wqr[:, :, :, :, :C].reshape(C, C)
        tokens = hid[:, :, here, b].reshape(256, C)
        grown = jnp.dot(tokens, block, preferred_element_type=F32).astype(BF)
        qb[:, :, :, b] = grown.reshape(2, 4, 2, 16, C)

    def row_step(hp):
        for head in range(HEADS):
            cut = slice(head * DIM, (head + 1) * DIM)
            vcut = slice(C + head * DIM, C + (head + 1) * DIM)
            q = qb[hp, :, :, :, :, cut].reshape(4, 64, DIM)
            keys = kv[hp, :, :, :, :, cut].reshape(4, 128, DIM)
            values = kv[hp, :, :, :, :, vcut].reshape(4, 128, DIM)
            mixed[pl.ds(0, 256), cut] = attend(q, keys, values).astype(BF)

        block = wor[...].reshape(C, C)
        grown = jnp.dot(mixed[pl.ds(0, 256), :], block, preferred_element_type=F32)
        grown = (grown + hid[hp, :, here].reshape(256, C).astype(F32)).reshape(4, 64, C)
        for d in range(8):
            send[hp, d] = grown[:, d * 8 : (d + 1) * 8, :].reshape(32, C).astype(BF)

        for dy in (2, 1, 3, 0):
            for dc in range(2):
                if dy == 0 and dc == 0:
                    continue
                ty, tc = (y + dy) % 4, (c + dc) % 2
                push(
                    send.at[hp, ty * 2 + tc], cols.at[hp, yc], s_a2a.at[hp, dy * 2 + dc], at(y=ty, c=tc)
                )
        return pull(send.at[hp, yc], cols.at[hp, yc])

    def row_arrived(hp):
        for dy in (2, 1, 3, 0):
            for dc in range(2):
                if dy == 0 and dc == 0:
                    continue
                sy, sc = (y + 4 - dy) % 4, (c + dc) % 2
                arrived(cols.at[hp, sy * 2 + sc], s_a2a.at[hp, dy * 2 + dc])

    reduce_x(0)
    mirror_send(0, 0)
    near_y(0, 0)
    mirror_send(0, 1)
    mirror_pass(0, 0)
    reduce_x_arrived(0)
    reduce_x(1)
    slab_copy.wait()
    reduce_z(0)
    mirror_pass(0, 1)
    mirror_send(1, 0)
    mirror_send(1, 1)
    gather_x(0)
    near_y(0, 1)
    near_y(1, 0)
    near_x(0, 0)
    reduce_x_arrived(1)
    reduce_z(1)
    gather_x_arrived(0)
    ring_send(1, 0)
    mirror_pass(1, 0)
    mirror_pass(1, 1)
    gather_x(1)
    near_y(1, 1)
    near_x(0, 1)
    ring_arrived(1, 0)
    ring_send(2, 0)
    gather_x_arrived(1)
    ring_send(1, 1)
    far_y(1, 0, 0)
    near_x(1, 0)
    ring_arrived(2, 0)
    ring_send(3, 0)
    ring_arrived(1, 1)
    ring_send(2, 1)
    near_x(1, 1)
    near_d(0, 0)
    far_y(1, 0, 1)
    ring_arrived(3, 0)
    ring_send(4, 0)
    ring_arrived(2, 1)
    ring_send(3, 1)
    near_d(0, 1)
    far_f(1, 0, 0)
    far_y(1, 1, 0)
    far_y(1, 1, 1)
    ring_arrived(4, 0)
    ring_arrived(3, 1)
    ring_send(4, 1)
    near_d(1, 0)
    near_d(1, 1)
    far_f(1, 0, 1)
    for copy in table_copies:
        copy.wait()
    time = lead_ids[0]
    film_gain = 1.0 + scale_t[pl.ds(time, 1), :]
    film_bias = shift_t[pl.ds(time, 1), :]
    weights_ready(0, 0)
    project(0)
    far_x(1, 0, 0)
    far_x(1, 0, 1)
    far_f(1, 1, 0)
    far_f(1, 1, 1)
    ring_arrived(4, 1)
    project(1)
    far_x(1, 1, 0)
    far_x(1, 1, 1)
    far_d(1, 0)
    weights_ready(0, 1)
    own0 = row_step(0)
    far_d(1, 1)
    own1 = row_step(1)
    def prepare(hp):
        @pl.loop(0, 8)
        def _(i):
            part = cols[hp, i].astype(F32)
            part = part * lax.rsqrt(jnp.mean(part * part, axis=-1, keepdims=True) + 1e-06) * gain[...]
            rows = pl.ds(pl.multiple_of(hp * 256 + i * 32, 32), 32)
            for s in range(8):
                xf[s, rows, :] = part[:, s * DIM : (s + 1) * DIM]

        for w in range(8):
            for s in range(8):
                taken = xf[s, pl.ds(hp * 256 + w, 32, stride=8), :]
                xt[hp, w * 32 : (w + 1) * 32, s * DIM : (s + 1) * DIM] = taken.astype(BF)

        grown = jnp.dot(xt[hp], wqc[...].reshape(C, 3 * C), preferred_element_type=F32).astype(BF)
        kvc[:, hp] = grown.reshape(8, 32, 3 * C)

    own0.wait()
    row_arrived(0)
    weights_ready(1, 0)
    prepare(0)
    own1.wait()
    row_arrived(1)
    prepare(1)

    for head in range(HEADS):
        cut = slice(head * DIM, (head + 1) * DIM)
        q, keys, values = (
            kvc[:, :, :, i * C + head * DIM : i * C + (head + 1) * DIM].reshape(8, 64, DIM) for i in range(3)
        )
        mix = attend(q, keys, values)
        for w in range(8):
            xf[head, pl.ds(w, 64, stride=8), :] = mix[w * 64 : (w + 1) * 64]
        mixed[:, cut] = xf[head].astype(BF)

    weights_ready(1, 1)
    block = woc[...].reshape(C, C)
    written = []
    for hp in range(2):
        rows = pl.ds(hp * 256, 256)
        grown = jnp.dot(mixed[rows, :], block, preferred_element_type=F32)
        stage[rows, :] = (grown + cols[hp].reshape(256, C).astype(F32)).astype(BF)
        written.append(pull(stage.at[rows], out.at[rows]))
    for copy in written:
        copy.wait()

    for copy in started:
        copy.wait_send()

    @pl.when(edge)
    def _():
        for a in range(2):
            for j in range(2):
                for forward in (False, True):
                    edge_copy(a, j, forward).wait_send()


def on_device(
    latents, owners, lead_ids, film_scale, film_shift, w_qkv_row, w_out_row, gain_col, w_qkv_col, w_out_col
):
    anywhere = pl.BlockSpec(memory_space=pl.ANY)
    scalars = pl.BlockSpec(memory_space=pltpu.SMEM)
    vector = pl.BlockSpec(memory_space=pltpu.VMEM)
    dma = pltpu.SemaphoreType.DMA
    result = pl.pallas_call(
        kernel,
        out_shape=jax.ShapeDtypeStruct((512, C), BF),
        in_specs=[
            anywhere, scalars, scalars, anywhere, anywhere, anywhere, anywhere, vector, anywhere, anywhere
        ],
        out_specs=anywhere,
        scratch_shapes=[
            pltpu.VMEM((512, C), BF),
            pltpu.VMEM((4, 2, 16, C), BF),
            pltpu.VMEM((360, C), F32),
            pltpu.VMEM((360, C), F32),
            pltpu.VMEM((3, 4, 2, 16, C), BF),
            pltpu.VMEM((4, 2, 16, C), BF),
            pltpu.VMEM((3, 2, 16, C), BF),
            pltpu.VMEM((2, 4, 4, 2, 16, C), BF),
            pltpu.VMEM((2, 4, 4, 2, 16, C), BF),
            pltpu.VMEM((2, 256, C), BF),
            pltpu.VMEM((2, 4, 4, 2, 16, 2 * C), BF),
            pltpu.VMEM((8, 2, 32, 3 * C), BF),
            pltpu.VMEM((2, 4, 2, 2, 16, C), BF),
            pltpu.VMEM((512, C), BF),
            pltpu.VMEM((2, 8, 32, C), BF),
            pltpu.VMEM((2, 8, 32, C), BF),
            pltpu.VMEM((8, 512, DIM), F32),
            pltpu.VMEM((2, 4, 2, 64, 3 * C), BF),
            pltpu.VMEM((2, 4, 2, 64, C), BF),
            pltpu.VMEM((2, 4, 2, 64, 3 * C), BF),
            pltpu.VMEM((2, 4, 2, 64, C), BF),
            dma((SENDS,)),
            dma((11,)),
            dma((2, 3)),
            dma((2, 3)),
            dma((2, 3)),
            dma((2, 4, 2)),
            dma((2, 2, 2)),
            dma((2, 2, 3)),
            dma((2, 2)),
            dma((2, 2, 2, 2)),
            dma((2, 2, 2, 2)),
            dma((2, 2, 2, 2, 4)),
            dma((2, 2, 2, 2)),
            dma((2, 8)),
        ],
        compiler_params=pltpu.CompilerParams(
            collective_id=0, has_side_effects=True, vmem_limit_bytes=56 << 20
        ),
        name="axial_attention",
    )(
        latents.reshape(4, 4, 2, 16, C), owners, lead_ids, film_scale, film_shift,
        w_qkv_row, w_out_row, gain_col.reshape(1, C), w_qkv_col, w_out_col,
    )
    return result.reshape(1, 64, 8, C)


def solution(mesh):
    placed = (
        P("lead", "space", None, None),
        P(),
        P("lead"),
        P(),
        P(),
        P("space", None),
        P("space", None),
        P(),
        P("space", None),
        P("space", None),
    )
    return jax.shard_map(
        on_device,
        mesh=mesh,
        in_specs=placed,
        out_specs=P("lead", None, "space", None),
        check_vma=False,
    )
```
